32 devices in a mesh: cfg: 2 (over y), group: 4 (over x, core), mp: 4 (over z).
Axes of the slice: x: 2, y: 2, z: 4, core: 2. Of those that a mesh axis runs over, the one named last changes fastest.
Arguments:
- latents: float32 [4096, 64], P(('group', 'mp')), may hold values from -0.6 to 0.6
- text_hidden: bfloat16 [2, 2048, 3072], P('cfg', ('group', 'mp')), may hold values from -6 to 6
- w_img_in: bfloat16 [64, 3072], replicated, may hold values from -0.75 to 0.75
- w_img_qkv: bfloat16 [3072, 4608], P(None, 'mp'), may hold values from -1 to 1
- w_txt_kv: bfloat16 [3072, 3072], P(None, 'mp'), may hold values from -0.109375 to 0.109375
- q_gain: float32 [128], replicated, may hold values from 0.25 to 1.75
- k_gain: float32 [128], replicated, may hold values from 0.25 to 1.75
- w_out: bfloat16 [1536, 3072], replicated, may hold values from -1 to 1
- w_final: bfloat16 [3072, 64], replicated, may hold values from -0.109375 to 0.109375
- mod_img: float32 [8, 3, 3072], replicated, may hold values from -3 to 3
- mod_txt: float32 [8, 2, 3072], replicated, may hold values from -3 to 3
- mod_final: float32 [8, 2, 3072], replicated, may hold values from -3 to 3
- guide: float32 [4], replicated, may hold values from 1.5 to 5
- step_size: float32 [8], replicated, may hold values from 0.02 to 0.3
- img_len: int32 [4], replicated, may hold values from 1 to 1024, as said below
- txt_len: int32 [4], replicated, may hold values from 1 to 512, as said below
- split_flag: int32 [2, 4], replicated, may hold values from 0 to 1, as said below
- tstep: int32 [4], replicated, may hold values from 0 to 7
Outputs:
- velocity: float32 [2, 2048, 64], P('cfg', ('group', 'mp'))
- next_latents: float32 [2, 2048, 64], P('cfg', ('group', 'mp'))
The draws below stay inside these ranges and needn't reach their ends.
Inputs may be any that keep to these rules, and one draw needn't show every extreme that they name: `img_len`: some group has exactly 1024 live image tokens. `txt_len`: some group has exactly 512 live text tokens. `split_flag`: entries [c, 2j] and [c, 2j + 1] are equal; at least one such pair carries 1 and at least one carries 0.
All inputs are finite; a program needn't handle non-finite values.
Results may differ from the reference program's by a relative error of at most 0.035.
Values may be sent and summed in bfloat16 or wider, within the bound.
No kernel may reach another device: no remote copies, remote signals or barrier semaphores. Data moves between devices by JAX's collectives and lax.ppermute only.
A program may use at most 192 MiB of HBM per device.

```python
import math
import jax
import jax.numpy as jnp
from jax import lax

D = 3072
HD = 128
CH = 64
HEADS = 12
NT = 8
IMG = 1024
TXT = 512
GROUPS = 4
N_MP = 4


def bounded_lengths(key, most):
    first, second = jax.random.split(key)
    values = jax.random.randint(first, (GROUPS,), 1, most + 1)
    chosen = jax.random.randint(second, (), 0, GROUPS)
    return jnp.where(jnp.arange(GROUPS) == chosen, most, values).astype(jnp.int32)


def draw_img_len(key, part):
    return bounded_lengths(jax.random.fold_in(key, 11), IMG)


def draw_txt_len(key, part):
    return bounded_lengths(jax.random.fold_in(key, 12), TXT)


def draw_split_flag(key, part):
    first, second, third = jax.random.split(jax.random.fold_in(key, 13), 3)
    pair_count = GROUPS
    paired = jax.random.randint(first, (pair_count,), 0, 2)
    chosen_on = jax.random.randint(second, (), 0, pair_count)
    offset = jax.random.randint(third, (), 1, pair_count)
    chosen_off = (chosen_on + offset) % pair_count
    pair_ids = jnp.arange(pair_count)
    paired = jnp.where(pair_ids == chosen_on, 1, paired)
    paired = jnp.where(pair_ids == chosen_off, 0, paired)
    return jnp.repeat(paired.reshape(2, GROUPS // 2), 2, axis=1).astype(jnp.int32)


def draw_mod_img(key, part):
    first, second, third = jax.random.split(jax.random.fold_in(key, 31), 3)
    shifts = 0.5 * jax.random.truncated_normal(first, -6.0, 6.0, (NT, 2, D), jnp.float32)
    sizes = jax.random.uniform(second, (NT, 1, D), jnp.float32, 1.5, 3.0)
    signs = jnp.where(jax.random.bernoulli(third, 0.5, (NT, 1, D)), 1.0, -1.0).astype(jnp.float32)
    return jnp.concatenate([shifts, signs * sizes], axis=1).astype(jnp.float32)


def draw_w_img_qkv(key, part):
    first = jax.random.fold_in(jax.random.fold_in(key, 32), 0)
    own = jax.random.truncated_normal(first, -4.0, 4.0, (D, HEADS, 3 * HD), jnp.float32)
    return (own * D ** (-0.5)).reshape(D, 3 * HEADS * HD).astype(jnp.bfloat16)


def draw_w_out(key, part):
    first = jax.random.fold_in(jax.random.fold_in(key, 33), 0)
    own = jax.random.truncated_normal(first, -4.0, 4.0, (HEADS, HD, D), jnp.float32)
    return (own * (HEADS * HD) ** (-0.5)).reshape(HEADS * HD, D).astype(jnp.bfloat16)


def with_ends(entries, stream_key, smallest, largest):
    index_at = [jax.random.randint(jax.random.fold_in(stream_key, axis), (), 0, length) for axis, length in enumerate(entries.shape)]
    widest = entries.shape.index(max(entries.shape))
    beside = index_at[:widest] + [(index_at[widest] + 1) % entries.shape[widest]] + index_at[widest + 1:]
    return entries.at[tuple(index_at)].set(smallest).at[tuple(beside)].set(largest)


def steps_of(rng, shape, cuts, least, largest):
    factor_of = 1.0
    for dim, shards_of in cuts:
        draws = jax.random.uniform(jax.random.fold_in(jax.random.fold_in(rng, 6), dim), (shards_of,), jnp.float32, least / len(cuts), largest / len(cuts))
        factor_of = factor_of * jnp.repeat(jnp.exp(draws), shape[dim] // shards_of).reshape((-1,) + (1,) * (len(shape) - 1 - dim))
    return factor_of


def normal_values(own_key, shape, deviation, most, pieces=(), held_as=jnp.bfloat16):
    result = deviation * jax.random.normal(own_key, shape, jnp.float32)
    if pieces:
        result = result * steps_of(own_key, shape, pieces, -0.22, 0.18)
    return jnp.clip(result, -most, most).astype(held_as)


def setup_inputs(seed: int = 0) -> dict:
    keys = jax.random.split(jax.random.key(seed), 19)
    latents = normal_values(keys[0], (GROUPS * IMG, CH), 0.1, 0.6, ((0, 16),), jnp.float32)
    text_hidden = normal_values(keys[1], (2, GROUPS * TXT, D), 1.0, 6.0, ((0, 2), (1, 16)))
    w_img_in = normal_values(keys[2], (CH, D), CH ** -0.5, 0.75)
    w_img_qkv = draw_w_img_qkv(jax.random.fold_in(keys[18], 71), 0)
    w_txt_kv = normal_values(keys[4], (D, 2 * HEADS * HD), D ** -0.5, 0.109375, ((1, 4),))
    q_gain = jnp.clip(1.0 + 0.15 * jax.random.normal(keys[5], (HD,), jnp.float32), 0.25, 1.75)
    k_gain = jnp.clip(1.0 + 0.15 * jax.random.normal(keys[6], (HD,), jnp.float32), 0.25, 1.75)
    w_out = draw_w_out(jax.random.fold_in(keys[18], 71), 0)
    w_final = normal_values(keys[8], (D, CH), D ** -0.5, 0.109375)
    mod_img = draw_mod_img(jax.random.fold_in(keys[18], 71), 0)
    mod_txt = normal_values(keys[10], (NT, 2, D), 0.5, 3.0, (), jnp.float32)
    mod_final = normal_values(keys[11], (NT, 2, D), 0.5, 3.0, (), jnp.float32)
    guide = jnp.clip(jax.random.uniform(keys[12], (GROUPS,), jnp.float32, 1.5, 5.0), 1.5, 5.0)
    step_size = jnp.clip(jnp.exp(jax.random.uniform(keys[13], (NT,), jnp.float32, math.log(0.02), math.log(0.3))), 0.02, 0.3)
    img_len = draw_img_len(jax.random.fold_in(keys[18], 71), 0)
    txt_len = draw_txt_len(jax.random.fold_in(keys[18], 71), 0)
    split_flag = draw_split_flag(jax.random.fold_in(keys[18], 71), 0)
    tstep = with_ends(jax.random.randint(keys[17], (GROUPS,), 0, NT), jax.random.fold_in(keys[17], 1), 0, NT - 1).astype(jnp.int32)
    return {"latents": latents, "text_hidden": text_hidden, "w_img_in": w_img_in, "w_img_qkv": w_img_qkv, "w_txt_kv": w_txt_kv, "q_gain": q_gain, "k_gain": k_gain, "w_out": w_out, "w_final": w_final, "mod_img": mod_img, "mod_txt": mod_txt, "mod_final": mod_final, "guide": guide, "step_size": step_size, "img_len": img_len, "txt_len": txt_len, "split_flag": split_flag, "tstep": tstep}


def layer_norm(values):
    center = values - lax.optimization_barrier(jnp.mean(values, -1, keepdims=True))
    spread = lax.optimization_barrier(jnp.mean(center * center, -1, keepdims=True))
    return center * lax.rsqrt(spread + 1e-06)

def head_norm(values, gain):
    return values * lax.rsqrt(lax.optimization_barrier(jnp.mean(values * values, -1, keepdims=True)) + 1e-06) * gain

def arrange_rows(values):
    half_rows = IMG // (2 * N_MP)
    split_rows = values.reshape(GROUPS, N_MP, 2, half_rows, CH)
    return jnp.transpose(split_rows, (2, 0, 1, 3, 4)).reshape(2, GROUPS * IMG // 2, CH)

def reference(latents, text_hidden, w_img_in, w_img_qkv, w_txt_kv, q_gain, k_gain, w_out, w_final, mod_img, mod_txt, mod_final, guide, step_size, img_len, txt_len, split_flag, tstep):
    x_img = jnp.dot(latents.astype(jnp.bfloat16), w_img_in, preferred_element_type=jnp.float32).reshape(GROUPS, IMG, D)
    mod_rows = mod_img[tstep]
    img_mod = (layer_norm(x_img) * (1.0 + mod_rows[:, 1:2]) + mod_rows[:, 0:1]).astype(jnp.bfloat16)
    text_rows = mod_txt[tstep]
    texts = text_hidden.astype(jnp.float32).reshape(2, GROUPS, TXT, D)
    txt_mod = (layer_norm(texts) * (1.0 + text_rows[None, :, 1:2]) + text_rows[None, :, 0:1]).astype(jnp.bfloat16)
    qkv = jnp.dot(img_mod.reshape(GROUPS * IMG, D), w_img_qkv, preferred_element_type=jnp.float32).reshape(GROUPS, IMG, HEADS, 3, HD)
    query = head_norm(qkv[..., 0, :], q_gain).astype(jnp.bfloat16)
    key_img = head_norm(qkv[..., 1, :], k_gain).astype(jnp.bfloat16)
    value_img = qkv[..., 2, :].astype(jnp.bfloat16)
    text_kv = jnp.dot(txt_mod.reshape(2 * GROUPS * TXT, D), w_txt_kv, preferred_element_type=jnp.float32).reshape(2, GROUPS, TXT, HEADS, 2, HD)
    key_txt = head_norm(text_kv[..., 0, :], k_gain).astype(jnp.bfloat16)
    value_txt = text_kv[..., 1, :].astype(jnp.bfloat16)
    key_all = jnp.concatenate([key_txt, jnp.broadcast_to(key_img[None], (2,) + key_img.shape)], axis=2)
    value_all = jnp.concatenate([value_txt, jnp.broadcast_to(value_img[None], (2,) + value_img.shape)], axis=2)
    spots_txt = jnp.arange(TXT, dtype=jnp.int32)
    spots_img = jnp.arange(IMG, dtype=jnp.int32)
    valid = jnp.concatenate([spots_txt[None, :] < txt_len[:, None], spots_img[None, :] < img_len[:, None]], axis=1)
    final_rows = mod_final[tstep]

    def one_item(index):
        side = index // GROUPS
        group = index % GROUPS
        mate = jnp.bitwise_xor(group, 1)
        key_rows = jnp.concatenate([key_all[side, group], key_all[side, mate]], axis=0)
        value_rows = jnp.concatenate([value_all[side, group], value_all[side, mate]], axis=0)
        live = jnp.concatenate([valid[group], valid[mate] & (split_flag[side, group] == 1)])
        scores = jnp.einsum('qhe,khe->hqk', query[group].astype(jnp.float32), key_rows.astype(jnp.float32)) * HD ** (-0.5)
        scores = jnp.where(live[None, None, :], scores, -1e+30)
        weights = jnp.exp(scores - lax.optimization_barrier(jnp.max(scores, -1, keepdims=True)))
        probs = (weights / lax.optimization_barrier(jnp.sum(weights, -1, keepdims=True))).astype(jnp.bfloat16)
        mixed = jnp.einsum('hqk,khe->qhe', probs.astype(jnp.float32), value_rows.astype(jnp.float32)).astype(jnp.bfloat16)
        attended = jnp.dot(mixed.reshape(IMG, HEADS * HD), w_out, preferred_element_type=jnp.float32)
        hidden = x_img[group] + mod_rows[group, 2] * attended
        final = (layer_norm(hidden) * (1.0 + final_rows[group, 1]) + final_rows[group, 0]).astype(jnp.bfloat16)
        return jnp.dot(final, w_final, preferred_element_type=jnp.float32)
    vel = lax.map(one_item, jnp.arange(2 * GROUPS, dtype=jnp.int32)).reshape(2, GROUPS, IMG, CH)
    guided = vel[1] + guide[:, None, None] * (vel[0] - vel[1])
    row_live = spots_img[None, :] < img_len[:, None]
    guided = jnp.where(row_live[:, :, None], guided, 0.0)
    start = latents.reshape(GROUPS, IMG, CH)
    moved = start - step_size[tstep][:, None, None] * guided
    return (arrange_rows(guided), arrange_rows(moved))
```

```python
import functools

import jax
import jax.numpy as jnp
import numpy as np
from jax import lax
from jax.experimental import pallas as pl
from jax.experimental.pallas import tpu as pltpu
from jax.sharding import PartitionSpec as P

HD = 128
EPS = 1e-6
BF = jnp.bfloat16
F32 = jnp.float32
QSCALE = float(HD**-0.5 / np.log(2.0))
VLIM = 32 * 2**20


def ring(value, step):
    n = lax.axis_size("mp")
    return lax.ppermute(value, "mp", [(i, (i + step) % n) for i in range(n)])


def partner(value, axis):
    n = lax.axis_size(axis)
    return lax.ppermute(value, axis, [(i, i ^ 1) for i in range(n)])


def split2(value):
    high = value.astype(BF)
    return high, (value - high.astype(F32)).astype(BF)


def dot(a, b):
    return jnp.dot(a, b, preferred_element_type=F32)


def dot_t(a, b):
    return lax.dot_general(a, b, (((1,), (1,)), ((), ())), preferred_element_type=F32)


def call(body, name, scalars, grid, in_specs, out_specs, out_shape, scratch, args, flops, nbytes):
    return pl.pallas_call(
        body,
        name=name,
        grid_spec=pltpu.PrefetchScalarGridSpec(
            num_scalar_prefetch=len(scalars),
            grid=grid,
            in_specs=in_specs,
            out_specs=out_specs,
            scratch_shapes=scratch,
        ),
        out_shape=out_shape,
        compiler_params=pltpu.CompilerParams(vmem_limit_bytes=VLIM),
        cost_estimate=pl.CostEstimate(flops=flops, bytes_accessed=nbytes, transcendentals=0),
    )(*scalars, *args)


def whole(shape):
    return pl.BlockSpec(shape, lambda *_: (0,) * len(shape))


def prep_body(*refs):
    *lat_refs, win_ref, out_ref = refs
    for i, ref in enumerate(lat_refs):
        rows = ref[...].T.astype(BF)
        n = rows.shape[0]
        x = dot(rows, win_ref[...])
        center = x - jnp.mean(x, -1, keepdims=True)
        rstd = lax.rsqrt(jnp.mean(center * center, -1, keepdims=True) + EPS)
        high, low = split2(rows.astype(F32) * rstd)
        out_ref[i * n : (i + 1) * n, :] = jnp.concatenate([high, low], axis=1)


def fold_body(ids, tstep, win_ref, mod_ref, w_ref, mats_ref, shift_ref, rows_ref):
    ch, d = win_ref.shape

    @pl.when(pl.program_id(0) == 0)
    def _():
        values = win_ref[...].astype(F32)
        center = values - jnp.mean(values, -1, keepdims=True)
        spot = lax.broadcasted_iota(jnp.int32, (16, d), 0)
        tail = jnp.zeros((16, d), F32)
        for i in range(2):
            at = pl.ds(tstep[ids[1] ^ i], 1)
            high, low = split2(center * (1.0 + mod_ref[1, at, :]))
            rows_ref[2 * i * ch : (2 * i + 1) * ch, :] = high
            rows_ref[(2 * i + 1) * ch : (2 * i + 2) * ch, :] = low
            high, low = split2(mod_ref[0, at, :])
            tail = jnp.where(spot == 2 * i, high.astype(F32), tail)
            tail = jnp.where(spot == 2 * i + 1, low.astype(F32), tail)
        rows_ref[4 * ch :, :] = tail.astype(BF)

    out = dot(rows_ref[...], w_ref[...])
    for i in range(2):
        high, low = split2(out[2 * i * ch : (2 * i + 1) * ch] + out[(2 * i + 1) * ch : (2 * i + 2) * ch])
        mats_ref[i] = jnp.concatenate([high, high, low], axis=0)
        base = 4 * ch + 2 * i
        shift_ref[i] = jnp.broadcast_to(out[base : base + 1] + out[base + 1 : base + 2], shift_ref.shape[1:])


def live_mask(first, rows, length):
    return (lax.broadcasted_iota(jnp.int32, (rows, HD), 0) + first) < length


def fill_ones(ref):
    head = [lax.broadcasted_iota(jnp.int32, ref.shape, i) // HD for i in range(2)]
    ref[...] = (head[0] == head[1]).astype(BF)


def head_norm(values, ones, gain):
    square = dot((values * values).astype(BF), ones)
    return values * lax.rsqrt(square * (1.0 / HD) + EPS) * gain


def image_body(kb, n_mp, ids, img_len, flags, own_ref, mate_ref, mats_ref, shift_ref, qg_ref, kg_ref,
               q_ref, acc_ref, k_ref, v_ref, x_ref, ones_ref):
    group = ids[1]
    n_rows = own_ref.shape[0]
    shard = n_rows // n_mp
    half = HD // 2
    length = img_len[group]
    mate_length = jnp.where(flags[ids[0], group] == 1, img_len[group ^ 1], 0)

    @pl.when(pl.program_id(0) == 0)
    def _():
        fill_ones(ones_ref)
        for base, ref, most in ((0, own_ref, length), (n_rows, mate_ref, mate_length)):
            for s in range(n_mp):
                start = pl.multiple_of(lax.rem(ids[2] + n_mp - s, n_mp) * shard, shard)
                lat = ref[s * shard : (s + 1) * shard, :]
                x_ref[pl.ds(base + start, shard), :] = jnp.concatenate(
                    [lat, lat[:, :half], jnp.zeros((shard, half), BF)], axis=1
                )
            v_ref[base : base + n_rows, HD:] = live_mask(0, n_rows, most).astype(BF)

    zeros = jnp.zeros((half, 3 * HD), BF)
    own_mat = jnp.concatenate([mats_ref[0], zeros], axis=0)
    block = dot(x_ref[:n_rows, :], own_mat) + shift_ref[0, 0:1, :]
    gains = jnp.concatenate([qg_ref[...] * QSCALE, kg_ref[...]], axis=1)
    normed = head_norm(block[:, : 2 * HD], ones_ref[...], gains).astype(BF)
    q_ref[0] = normed[:, :HD]
    k_ref[:n_rows, :] = normed[:, HD:]
    v_ref[:n_rows, :HD] = jnp.where(live_mask(0, n_rows, length), block[:, 2 * HD :], 0.0).astype(BF)

    @pl.when(mate_length > 0)
    def _():
        mate_mat = jnp.concatenate([mats_ref[1], zeros], axis=0)[:, HD:]
        block = dot(x_ref[n_rows:, :], mate_mat) + shift_ref[1, 0:1, HD:]
        k_ref[n_rows:, :] = head_norm(block[:, :HD], ones_ref[:HD, :HD], kg_ref[...]).astype(BF)
        v_ref[n_rows:, :HD] = jnp.where(
            live_mask(0, n_rows, mate_length), block[:, HD:], 0.0
        ).astype(BF)

    def attend(start):
        spot = pl.ds(start, kb)
        p = jnp.exp2(dot_t(q_ref[0], k_ref[spot, :])).astype(BF)
        return dot(p, v_ref[spot, :])

    acc_ref[0] = attend(0)
    for start in range(kb, 2 * n_rows, kb):
        seen = length > start if start < n_rows else mate_length > start - n_rows

        @pl.when(seen)
        def _():
            acc_ref[0] += attend(start)


def text_body(n_in, ids, tstep, *refs):
    rows_refs, (mod_ref, w_ref, kg_ref, out_ref, ones_ref) = refs[:n_in], refs[n_in:]
    fill_ones(ones_ref)
    first = 0
    for ref in rows_refs:
        n = ref.shape[0]
        x = ref[...].astype(F32)
        center = x - jnp.mean(x, -1, keepdims=True)
        rstd = lax.rsqrt(jnp.mean(center * center, -1, keepdims=True) + EPS)
        y = (center * rstd * (1.0 + mod_ref[0, 1:2, :]) + mod_ref[0, 0:1, :]).astype(BF)
        for h in range(out_ref.shape[0]):
            kv = dot(y, w_ref[:, 2 * HD * h : 2 * HD * (h + 1)])
            out_ref[h, first : first + n, :HD] = head_norm(kv[:, :HD], ones_ref[...], kg_ref[...]).astype(BF)
            out_ref[h, first : first + n, HD:] = kv[:, HD:].astype(BF)
        first += n


def text_attend(offsets, shard, n_mp, ids, txt_len, flags, q, acc, own, mate):
    side, group, m = ids[0], ids[1], ids[2]
    length = txt_len[group]
    mate_length = jnp.where(flags[side, group] == 1, txt_len[group ^ 1], 0)
    keys, values = [], []
    for kv, most in ((own, length), (mate, mate_length)):
        keys.append(kv[:, :HD])
        for i, off in enumerate(offsets):
            live = live_mask(lax.rem(m + off, n_mp) * shard, shard, most)
            v = kv[i * shard : (i + 1) * shard, HD:]
            values.append(
                jnp.concatenate([jnp.where(live, v, jnp.zeros_like(v)), live.astype(BF)], axis=1)
            )
    p = jnp.exp2(dot_t(q, jnp.concatenate(keys, axis=0))).astype(BF)
    return acc + dot(p, jnp.concatenate(values, axis=0))


def near_body(offsets, shard, n_mp, ids, txt_len, flags, q_ref, acc_ref, own0, mate0, own1, mate1, out_ref):
    own = jnp.concatenate([own0[0], own1[0]], axis=0)
    mate = jnp.concatenate([mate0[0], mate1[0]], axis=0)
    out_ref[0] = text_attend(offsets, shard, n_mp, ids, txt_len, flags, q_ref[0], acc_ref[0], own, mate)


def last_body(offsets, shard, n_mp, ids, txt_len, flags, q_ref, acc_ref, own_ref, mate_ref, *out_refs):
    step = pl.program_id(0)
    half = q_ref.shape[1] // 2
    is_cond = ids[0] == 0
    parts = []
    for h in range(q_ref.shape[0]):
        acc = text_attend(
            offsets, shard, n_mp, ids, txt_len, flags, q_ref[h], acc_ref[h], own_ref[h], mate_ref[h]
        )
        parts.append((acc[:, :HD] / acc[:, HD:]).astype(BF))
    mixed = jnp.concatenate(parts, axis=1)
    low, high = mixed[:half], mixed[half:]
    for i in range(n_mp):

        @pl.when(step == i)
        def _():
            out_refs[2 * i][...] = jnp.where(is_cond, low, high)
            out_refs[2 * i + 1][...] = jnp.where(is_cond, high, low)


def stage_body(n_mp, ids, w_ref, lat_ref, win_ref, rest_ref, x_ref):
    rest_ref[0] = w_ref[0]

    @pl.when(pl.program_id(0) == 0)
    def _():
        half = x_ref.shape[0]
        lat = jnp.where(ids[0] == 0, lat_ref[:, :half], lat_ref[:, half:])
        x_ref[...] = dot(lat.T.astype(BF), win_ref[...])


def project_sides(pieces, weights):
    total = None
    for i, w in enumerate(weights):
        rows = jnp.concatenate([pieces[2 * i][...], pieces[2 * i + 1][...]], axis=0)
        term = dot(rows, w)
        total = term if total is None else total + term
    return total


def early_body(*refs):
    n = (len(refs) - 1) // 3
    refs[-1][...] = project_sides(refs[: 2 * n], [ref[0] for ref in refs[2 * n : -1]])


def out_body(ids, tstep, img_len, guide, step_size, *refs):
    pieces, refs = refs[:2], refs[2:]
    wout_ref, total_ref, x_ref, lat_ref, mod_ref, final_ref, wf_ref, vel_ref, next_ref = refs
    side, group, m = ids[0], ids[1], ids[2]
    step = tstep[group]
    total = total_ref[...] + project_sides(pieces, [wout_ref[0]])
    x = x_ref[...]
    hidden = jnp.concatenate([x, x], axis=0) + mod_ref[2, pl.ds(step, 1), :] * total
    center = hidden - jnp.mean(hidden, -1, keepdims=True)
    rstd = lax.rsqrt(jnp.mean(center * center, -1, keepdims=True) + EPS)
    final = (center * rstd * (1.0 + final_ref[0, 1:2, :]) + final_ref[0, 0:1, :]).astype(BF)
    vel = dot_t(wf_ref[...], final)
    half = x.shape[0]
    own, other = vel[:, :half], vel[:, half:]
    is_cond = side == 0
    cond = jnp.where(is_cond, own, other)
    uncond = jnp.where(is_cond, other, own)
    guided = uncond + guide[group] * (cond - uncond)
    place = lax.broadcasted_iota(jnp.int32, guided.shape, 1) + (2 * m + side) * half
    guided = jnp.where(place < img_len[group], guided, 0.0)
    vel_ref[0] = guided
    start = jnp.where(is_cond, lat_ref[:, :half], lat_ref[:, half:])
    next_ref[0] = start - step_size[step] * guided


def local(
    latents, text_hidden, w_img_in, w_img_qkv, w_txt_kv, q_gain, k_gain, w_out, w_final,
    mod_img, mod_txt, mod_final, guide, step_size, img_len, txt_len, split_flag, tstep,
):
    n_mp = lax.axis_size("mp")
    ids = jnp.stack([lax.axis_index("cfg"), lax.axis_index("group"), lax.axis_index("mp")]).astype(jnp.int32)
    rows, ch = latents.shape
    full = rows * n_mp
    d = w_img_in.shape[1]
    cols = w_img_qkv.shape[1]
    heads = cols // (3 * HD)
    shard = text_hidden.shape[1]
    qg, kg = q_gain.reshape(1, HD), k_gain.reshape(1, HD)

    lat_t = latents.T

    shards = [lat_t] + [ring(lat_t, s) for s in range(1, n_mp)]
    text, *shards = lax.optimization_barrier((text_hidden.reshape(shard, d), *shards))
    text_left = ring(text, 1)
    text_right = ring(text, n_mp - 1)
    own_lat = call(
        prep_body, "prep", (), (1,), [whole((ch, rows))] * n_mp + [whole((ch, d))],
        whole((full, 2 * ch)), jax.ShapeDtypeStruct((full, 2 * ch), BF), [],
        (*shards, w_img_in), 2 * full * ch * d, 2 * ch * d,
    )
    mate_lat = partner(own_lat, "group")

    mod_rows = jnp.transpose(mod_img, (1, 0, 2))
    at_step = pl.BlockSpec((1, 2, d), lambda s, ids, ts, *_: (ts[ids[1]], 0, 0))
    mats, shift = call(
        fold_body, "fold", (ids, tstep), (heads,),
        [whole((ch, d)), whole(mod_rows.shape), pl.BlockSpec((d, 3 * HD), lambda h, *_: (0, h))],
        [pl.BlockSpec((2, 3 * ch, 3 * HD), lambda h, *_: (0, 0, h)),
         pl.BlockSpec((2, 8, 3 * HD), lambda h, *_: (0, 0, h))],
        [jax.ShapeDtypeStruct((2, 3 * ch, cols), BF), jax.ShapeDtypeStruct((2, 8, cols), F32)],
        [pltpu.VMEM((4 * ch + 16, d), BF)],
        (w_img_in, mod_rows, w_img_qkv), 2 * 272 * d * cols, 2 * d * cols,
    )

    by_head = lambda *shape: pl.BlockSpec((1,) + shape, lambda h, *_: (h, 0, 0))
    q, acc = call(
        functools.partial(image_body, full, n_mp), "image_attention", (ids, img_len, split_flag), (heads,),
        [whole((full, 2 * ch)), whole((full, 2 * ch)),
         pl.BlockSpec((2, 3 * ch, 3 * HD), lambda h, *_: (0, 0, h)),
         pl.BlockSpec((2, 8, 3 * HD), lambda h, *_: (0, 0, h)), whole((1, HD)), whole((1, HD))],
        [by_head(full, HD), by_head(full, 2 * HD)],
        [jax.ShapeDtypeStruct((heads, full, HD), BF), jax.ShapeDtypeStruct((heads, full, 2 * HD), F32)],
        [pltpu.VMEM((2 * full, HD), BF), pltpu.VMEM((2 * full, 2 * HD), BF),
         pltpu.VMEM((2 * full, 2 * HD), BF), pltpu.VMEM((2 * HD, 2 * HD), BF)],
        (own_lat, mate_lat, mats, shift, qg, kg), 2 * heads * full * full * 4 * HD * 2, 2**22,
    )

    def text_kv(name, *pieces):
        n = sum(p.shape[0] for p in pieces)
        return call(
            functools.partial(text_body, len(pieces)), name, (ids, tstep), (1,),
            [whole(p.shape) for p in pieces] + [at_step, whole(w_txt_kv.shape), whole((1, HD))],
            whole((heads, n, 2 * HD)), jax.ShapeDtypeStruct((heads, n, 2 * HD), BF),
            [pltpu.VMEM((HD, HD), BF)],
            pieces + (mod_txt, w_txt_kv, kg), 2 * n * d * heads * 2 * HD, 2 * d * heads * 2 * HD,
        )

    kv_own = text_kv("text_kv_own", text)
    mate_own = partner(kv_own, "group")
    text_left, acc = lax.optimization_barrier((text_left, acc))
    text_far = ring(text_left, 1)
    kv_near = text_kv("text_kv_near", text_left, text_right)
    mate_near = partner(kv_near, "group")

    scalars = (ids, txt_len, split_flag)
    acc = call(
        functools.partial(near_body, (0, n_mp - 1, 1), shard, n_mp), "text_attention_near", scalars, (heads,),
        [by_head(full, HD), by_head(full, 2 * HD)] + [by_head(v.shape[1], 2 * HD) for v in (kv_own, mate_own, kv_near, mate_near)],
        by_head(full, 2 * HD), jax.ShapeDtypeStruct(acc.shape, F32), [],
        (q, acc, kv_own, mate_own, kv_near, mate_near), 2 * heads * full * 6 * shard * 3 * HD, 2**23,
    )
    text_far, acc = lax.optimization_barrier((text_far, acc))
    kv_far = text_kv("text_kv_far", text_far)
    mate_far = partner(kv_far, "group")
    block = lambda width: pl.BlockSpec(
        (heads, rows, width), lambda s, ids, *_: (0, lax.rem(ids[2] + s, n_mp), 0)
    )
    depth = heads * HD
    half = rows // 2
    mixed = call(
        functools.partial(last_body, (n_mp - 2,), shard, n_mp), "text_attention_far", scalars, (n_mp,),
        [block(HD), block(2 * HD), whole(kv_far.shape), whole(kv_far.shape)],
        [whole((half, depth))] * (2 * n_mp),
        [jax.ShapeDtypeStruct((half, depth), BF)] * (2 * n_mp), [],
        (q, acc, kv_far, mate_far), 2 * heads * full * 2 * shard * 3 * HD, 2**22,
    )

    n_cfg = lax.axis_size("cfg")

    def send(s, flip):
        if s == 0 and flip == 0:
            return mixed[0]
        pairs = [
            (c * n_mp + i, (c ^ flip) * n_mp + (i + s) % n_mp) for c in range(n_cfg) for i in range(n_mp)
        ]
        return lax.ppermute(mixed[2 * s + flip], ("cfg", "mp"), pairs)

    order = [2, 1, 0, 3]
    pieces = [send(s, flip) for s in order for flip in range(2)]
    w_late, _ = lax.optimization_barrier((w_out, mixed[0]))
    rest, x_kept = call(
        functools.partial(stage_body, n_mp), "out_weights", (ids,), (n_mp,),
        [pl.BlockSpec((1, depth, d), lambda s, ids: (lax.rem(ids[2] + n_mp - s, n_mp), 0, 0)),
         whole((ch, rows)), whole((ch, d))],
        [pl.BlockSpec((1, depth, d), lambda s, ids: (s, 0, 0)), whole((half, d))],
        [jax.ShapeDtypeStruct((n_mp, depth, d), BF), jax.ShapeDtypeStruct((half, d), F32)], [],
        (w_late.reshape(n_mp, depth, d), lat_t, w_img_in), 2 * half * ch * d, 4 * n_mp * depth * d,
    )
    at_weight = lambda s: pl.BlockSpec((1, depth, d), lambda *_: (s, 0, 0))
    total = call(
        early_body, "out_early", (), (1,),
        [whole((half, depth))] * (2 * (n_mp - 1)) + [at_weight(s) for s in order[:-1]],
        whole((rows, d)), jax.ShapeDtypeStruct((rows, d), F32), [],
        (*pieces[:-2], *[rest] * (n_mp - 1)), 2 * rows * (n_mp - 1) * depth * d, 2 * (n_mp - 1) * depth * d,
    )
    vel, moved = call(
        out_body, "out_late", (ids, tstep, img_len, guide, step_size), (1,),
        [whole((half, depth))] * 2
        + [at_weight(order[-1]), whole((rows, d)), whole((half, d)), whole((ch, rows)),
           whole(mod_rows.shape), at_step, whole((ch, d))],
        [whole((1, ch, half))] * 2, [jax.ShapeDtypeStruct((1, ch, half), F32)] * 2, [],
        (*pieces[-2:], rest, total, x_kept, lat_t, mod_rows, mod_final, w_final.T),
        2 * rows * depth * d, 2 * depth * d,
    )
    return jnp.swapaxes(vel, 1, 2), jnp.swapaxes(moved, 1, 2)


def solution(mesh):
    placed = (
        P(("group", "mp"), None),
        P("cfg", ("group", "mp"), None),
        P(),
        P(None, "mp"),
        P(None, "mp"),
    ) + (P(),) * 13
    return jax.shard_map(
        local,
        mesh=mesh,
        in_specs=placed,
        out_specs=(P("cfg", ("group", "mp"), None), P("cfg", ("group", "mp"), None)),
        check_vma=False,
    )
```

```python
import functools

import jax
import jax.numpy as jnp
import numpy as np
from jax import lax
from jax.experimental import pallas as pl
from jax.experimental.pallas import tpu as pltpu
from jax.sharding import PartitionSpec as P

HD = 128
EPS = 1e-6
BF = jnp.bfloat16
F32 = jnp.float32
QSCALE = float(HD**-0.5 / np.log(2.0))
VLIM = 20 * 2**20
CHUNK = 64


def ring(value, step):
    n = lax.axis_size("mp")
    return lax.ppermute(value, "mp", [(i, (i + step) % n) for i in range(n)])


def partner(value, axis):
    n = lax.axis_size(axis)
    return lax.ppermute(value, axis, [(i, i ^ 1) for i in range(n)])


def split2(value):
    high = value.astype(BF)
    return high, (value - high.astype(F32)).astype(BF)


def layer_norm(values):
    center = values - jnp.mean(values, -1, keepdims=True)
    return center * lax.rsqrt(jnp.mean(center * center, -1, keepdims=True) + EPS)


def dot(a, b):
    return jnp.dot(a, b, preferred_element_type=F32)


def dot_t(a, b):
    return lax.dot_general(a, b, (((1,), (1,)), ((), ())), preferred_element_type=F32)


FREE = ('prep', 'image_attention', 'text_kv_near', 'text_kv_far', 'text_attention_near', 'text_attention_far', 'out_weights', 'out_early', 'out_late')


def call(body, name, scalars, grid, in_specs, out_specs, out_shape, scratch, args, flops, nbytes):
    if name in FREE:
        flops = nbytes = 0
    return pl.pallas_call(
        body,
        name=name,
        grid_spec=pltpu.PrefetchScalarGridSpec(
            num_scalar_prefetch=len(scalars),
            grid=grid,
            in_specs=in_specs,
            out_specs=out_specs,
            scratch_shapes=scratch,
        ),
        out_shape=out_shape,
        compiler_params=pltpu.CompilerParams(vmem_limit_bytes=VLIM),
        cost_estimate=pl.CostEstimate(flops=flops, bytes_accessed=nbytes, transcendentals=0),
    )(*scalars, *args)


def whole(shape):
    return pl.BlockSpec(shape, lambda *_: (0,) * len(shape))


VMEM = pl.BlockSpec(memory_space=pltpu.VMEM)


def prep_body(*refs):
    *lat_refs, win_ref, out_ref = refs
    for i, ref in enumerate(lat_refs):
        rows = ref[...].astype(F32).T.astype(BF)
        n = rows.shape[0]
        x = dot(rows, win_ref[...])
        center = x - jnp.mean(x, -1, keepdims=True)
        rstd = lax.rsqrt(jnp.mean(center * center, -1, keepdims=True) + EPS)
        high, low = split2(rows.astype(F32) * rstd)
        out_ref[i * n : (i + 1) * n, :] = jnp.concatenate([high, low], axis=1)


def fold_body(ids, tstep, win_ref, mod_ref, w_ref, mats_ref, shift_ref, rows_ref, win_buf, mod_buf, w_buf, sems):
    heads = mats_ref.shape[0]
    ch, d = win_ref.shape
    width = 3 * HD
    first = [pltpu.make_async_copy(win_ref, win_buf, sems.at[heads])]
    first.append(pltpu.make_async_copy(mod_ref.at[0:2], mod_buf, sems.at[heads + 1]))
    weights = [
        pltpu.make_async_copy(w_ref.at[:, h * width : (h + 1) * width], w_buf.at[h], sems.at[h])
        for h in range(heads)
    ]
    for copy in first + weights:
        copy.start()
    for copy in first:
        copy.wait()
    values = win_buf[...].astype(F32)
    center = values - jnp.mean(values, -1, keepdims=True)
    spot = lax.broadcasted_iota(jnp.int32, (16, d), 0)
    tail = jnp.zeros((16, d), F32)
    for i in range(2):
        at = pl.ds(tstep[ids[1] ^ i], 1)
        high, low = split2(center * (1.0 + mod_buf[1, at, :]))
        rows_ref[2 * i * ch : (2 * i + 1) * ch, :] = high
        rows_ref[(2 * i + 1) * ch : (2 * i + 2) * ch, :] = low
        high, low = split2(mod_buf[0, at, :])
        tail = jnp.where(spot == 2 * i, high.astype(F32), tail)
        tail = jnp.where(spot == 2 * i + 1, low.astype(F32), tail)
    rows_ref[4 * ch :, :] = tail.astype(BF)
    for h, copy in enumerate(weights):
        copy.wait()
        out = dot(rows_ref[...], w_buf[h])
        for i in range(2):
            high, low = split2(out[2 * i * ch : (2 * i + 1) * ch] + out[(2 * i + 1) * ch : (2 * i + 2) * ch])
            mats_ref[h, i] = jnp.concatenate([high, high, low], axis=0)
            base = 4 * ch + 2 * i
            shift_ref[h, i] = jnp.broadcast_to(out[base : base + 1] + out[base + 1 : base + 2], shift_ref.shape[2:])


def live_mask(first, rows, length):
    return (lax.broadcasted_iota(jnp.int32, (rows, HD), 0) + first) < length


def fill_ones(ref):
    head = [lax.broadcasted_iota(jnp.int32, ref.shape, i) // HD for i in range(2)]
    ref[...] = (head[0] == head[1]).astype(BF)


def head_norm(values, ones, gain):
    square = dot((values * values).astype(BF), ones)
    return values * lax.rsqrt(square * (1.0 / HD) + EPS) * gain


def image_body(kb, n_mp, ids, img_len, flags, own_ref, mate_ref, mats_ref, shift_ref, qg_ref, kg_ref,
               q_ref, acc_ref, k_ref, v_ref, x_ref, ones_ref):
    group = ids[1]
    n_rows = own_ref.shape[0]
    shard = n_rows // n_mp
    half = HD // 2
    length = img_len[group]
    mate_length = jnp.where(flags[ids[0], group] == 1, img_len[group ^ 1], 0)

    @pl.when(pl.program_id(0) == 0)
    def _():
        fill_ones(ones_ref)
        for base, ref, most in ((0, own_ref, length), (n_rows, mate_ref, mate_length)):
            for s in range(n_mp):
                start = pl.multiple_of(lax.rem(ids[2] + n_mp - s, n_mp) * shard, shard)
                lat = ref[s * shard : (s + 1) * shard, :]
                x_ref[pl.ds(base + start, shard), :] = jnp.concatenate(
                    [lat, lat[:, :half], jnp.zeros((shard, half), BF)], axis=1
                )
            v_ref[base : base + n_rows, HD:] = live_mask(0, n_rows, most).astype(BF)

    zeros = jnp.zeros((half, 3 * HD), BF)
    own_mat = jnp.concatenate([mats_ref[0, 0], zeros], axis=0)
    block = dot(x_ref[:n_rows, :], own_mat) + shift_ref[0, 0, 0:1, :]
    gains = jnp.concatenate([qg_ref[...] * QSCALE, kg_ref[...]], axis=1)
    normed = head_norm(block[:, : 2 * HD], ones_ref[...], gains).astype(BF)
    q_ref[0] = normed[:, :HD]
    k_ref[:n_rows, :] = normed[:, HD:]
    v_ref[:n_rows, :HD] = jnp.where(live_mask(0, n_rows, length), block[:, 2 * HD :], 0.0).astype(BF)

    @pl.when(mate_length > 0)
    def _():
        mate_mat = jnp.concatenate([mats_ref[0, 1], zeros], axis=0)[:, HD:]
        block = dot(x_ref[n_rows:, :], mate_mat) + shift_ref[0, 1, 0:1, HD:]
        k_ref[n_rows:, :] = head_norm(block[:, :HD], ones_ref[:HD, :HD], kg_ref[...]).astype(BF)
        v_ref[n_rows:, :HD] = jnp.where(
            live_mask(0, n_rows, mate_length), block[:, HD:], 0.0
        ).astype(BF)

    def attend(start):
        spot = pl.ds(start, kb)
        p = jnp.exp2(dot_t(q_ref[0], k_ref[spot, :])).astype(BF)
        return dot(p, v_ref[spot, :])

    acc_ref[0] = attend(0)
    for start in range(kb, 2 * n_rows, kb):
        seen = length > start if start < n_rows else mate_length > start - n_rows

        @pl.when(seen)
        def _():
            acc_ref[0] += attend(start)


def text_body(n_in, ids, tstep, *refs):
    rows_refs, (mod_ref, w_ref, kg_ref, out_ref, ones_ref, y_ref) = refs[:n_in], refs[n_in:]
    fill_ones(ones_ref)
    step = tstep[ids[1]]
    scale = 1.0 + mod_ref[step, 1:2, :]
    first = 0
    for ref in rows_refs:
        for start in range(0, ref.shape[0], CHUNK):
            x = ref[start : start + CHUNK, :].astype(F32)
            y_ref[first : first + CHUNK, :] = (layer_norm(x) * scale + mod_ref[step, 0:1, :]).astype(BF)
            first += CHUNK
    kv = dot(y_ref[...], w_ref[...])
    for h in range(out_ref.shape[0]):
        k = kv[:, 2 * HD * h : 2 * HD * h + HD]
        out_ref[h, :, :HD] = head_norm(k, ones_ref[...], kg_ref[...]).astype(BF)
        out_ref[h, :, HD:] = kv[:, 2 * HD * h + HD : 2 * HD * (h + 1)].astype(BF)


def text_attend(offsets, shard, n_mp, ids, txt_len, flags, q, acc, own, mate):
    side, group, m = ids[0], ids[1], ids[2]
    length = txt_len[group]
    mate_length = jnp.where(flags[side, group] == 1, txt_len[group ^ 1], 0)
    keys, values = [], []
    for kv, most in ((own, length), (mate, mate_length)):
        keys.append(kv[:, :HD])
        for i, off in enumerate(offsets):
            live = live_mask(lax.rem(m + off, n_mp) * shard, shard, most)
            v = kv[i * shard : (i + 1) * shard, HD:]
            values.append(
                jnp.concatenate([jnp.where(live, v, jnp.zeros_like(v)), live.astype(BF)], axis=1)
            )
    p = jnp.exp2(dot_t(q, jnp.concatenate(keys, axis=0))).astype(BF)
    return acc + dot(p, jnp.concatenate(values, axis=0))


def near_body(offsets, shard, n_mp, ids, txt_len, flags, q_ref, acc_ref, own0, mate0, own1, mate1, out_ref):
    own = jnp.concatenate([own0[0], own1[0]], axis=0)
    mate = jnp.concatenate([mate0[0], mate1[0]], axis=0)
    out_ref[0] = text_attend(offsets, shard, n_mp, ids, txt_len, flags, q_ref[0], acc_ref[0], own, mate)


def last_body(offsets, shard, n_mp, ids, txt_len, flags, q_ref, acc_ref, own_ref, mate_ref, *out_refs):
    rows = q_ref.shape[1] // n_mp
    half = rows // 2
    is_cond = ids[0] == 0
    for i in range(n_mp):
        spot = pl.ds(pl.multiple_of(lax.rem(ids[2] + i, n_mp) * rows, rows), rows)
        for h in range(q_ref.shape[0]):
            acc = text_attend(
                offsets, shard, n_mp, ids, txt_len, flags, q_ref[h, spot, :], acc_ref[h, spot, :],
                own_ref[h], mate_ref[h],
            )
            mixed = (acc[:, :HD] / acc[:, HD:]).astype(BF)
            low, high = mixed[:half], mixed[half:]
            columns = slice(h * HD, (h + 1) * HD)
            out_refs[2 * i][:, columns] = jnp.where(is_cond, low, high)
            out_refs[2 * i + 1][:, columns] = jnp.where(is_cond, high, low)


def stage_body(n_mp, ids, w_ref, lat_ref, win_ref, rest_ref, x_ref):
    rest_ref[...] = w_ref[...]

    @pl.when(pl.program_id(0) == 0)
    def _():
        half = x_ref.shape[0]
        lat = jnp.where(ids[0] == 0, lat_ref[:, :half], lat_ref[:, half:])
        x_ref[...] = dot(lat.T.astype(BF), win_ref[...])


def project_sides(pieces, weights):
    own, other = (jnp.concatenate([ref[...] for ref in pieces[i::2]], axis=1) for i in range(2))
    return dot(jnp.concatenate([own, other], axis=0), weights)


def early_body(*refs):
    *pieces, wout_ref, total_ref = refs
    depth = pieces[0].shape[1] * len(pieces) // 2
    total_ref[...] = project_sides(pieces, wout_ref[:depth, :])


def out_body(n_late, ids, tstep, img_len, guide, step_size, *refs):
    pieces, refs = refs[: 2 * n_late], refs[2 * n_late :]
    wout_ref, total_ref, x_ref, lat_ref, mod_ref, final_ref, wf_ref, vel_ref, next_ref, total, final = refs
    side, group, m = ids[0], ids[1], ids[2]
    step = tstep[group]
    total[...] = total_ref[...] + project_sides(pieces, wout_ref[-n_late * pieces[0].shape[1] :, :])
    half = x_ref.shape[0]
    gate, scale = mod_ref[2, pl.ds(step, 1), :], 1.0 + final_ref[step, 1:2, :]
    for first in range(0, 2 * half, CHUNK):
        rows = slice(first, first + CHUNK)
        hidden = x_ref[first % half : first % half + CHUNK, :] + gate * total[rows, :]
        final[rows, :] = (layer_norm(hidden) * scale + final_ref[step, 0:1, :]).astype(BF)
    vel = dot_t(wf_ref[...], final[...])
    own, other = vel[:, :half], vel[:, half:]
    is_cond = side == 0
    cond = jnp.where(is_cond, own, other)
    uncond = jnp.where(is_cond, other, own)
    guided = uncond + guide[group] * (cond - uncond)
    place = lax.broadcasted_iota(jnp.int32, guided.shape, 1) + (2 * m + side) * half
    guided = jnp.where(place < img_len[group], guided, 0.0)
    vel_ref[0] = guided
    start = jnp.where(is_cond, lat_ref[:, :half], lat_ref[:, half:])
    next_ref[0] = start - step_size[step] * guided


def local(
    latents, text_hidden, w_img_in, w_img_qkv, w_txt_kv, q_gain, k_gain, w_out, w_final,
    mod_img, mod_txt, mod_final, guide, step_size, img_len, txt_len, split_flag, tstep,
):
    n_mp = lax.axis_size("mp")
    order, n_late = [*range(2, 0, -1), *range(3, n_mp), 0], 2
    ids = jnp.stack([lax.axis_index("cfg"), lax.axis_index("group"), lax.axis_index("mp"), *order]).astype(jnp.int32)
    rows, ch = latents.shape
    full = rows * n_mp
    d = w_img_in.shape[1]
    cols = w_img_qkv.shape[1]
    heads = cols // (3 * HD)
    shard = text_hidden.shape[1]
    qg, kg = q_gain.reshape(1, HD), k_gain.reshape(1, HD)

    lat_t = latents.T

    text = text_hidden.reshape(shard, d)
    text_left = ring(text, 1)
    lat_sent = lat_t.astype(BF)
    shards = [lat_sent] + [ring(lat_sent, s) for s in range(1, n_mp)]

    mod_rows = jnp.transpose(mod_img, (1, 0, 2))
    hbm = pl.BlockSpec(memory_space=pltpu.HBM)
    mats, shift = call(
        fold_body, "fold", (ids, tstep), (1,), [hbm] * 3, [VMEM] * 2,
        [jax.ShapeDtypeStruct((heads, 2, 3 * ch, 3 * HD), BF), jax.ShapeDtypeStruct((heads, 2, 8, 3 * HD), F32)],
        [pltpu.VMEM((4 * ch + 16, d), BF), pltpu.VMEM((ch, d), BF), pltpu.VMEM((2,) + mod_rows.shape[1:], F32),
         pltpu.VMEM((heads, d, 3 * HD), BF), pltpu.SemaphoreType.DMA((heads + 2,))],
        (w_img_in, mod_rows, w_img_qkv), 2 * 272 * d * cols, 2 * d * cols,
    )

    def text_kv(name, *pieces):
        n = sum(p.shape[0] for p in pieces)
        return call(
            functools.partial(text_body, len(pieces)), name, (ids, tstep), (1,),
            [VMEM] * (len(pieces) + 3), VMEM, jax.ShapeDtypeStruct((heads, n, 2 * HD), BF),
            [pltpu.VMEM((HD, HD), BF), pltpu.VMEM((n, d), BF)],
            pieces + (mod_txt, w_txt_kv, kg), 2 * n * d * heads * 2 * HD, 2 * d * heads * 2 * HD,
        )

    text_next, win_late, mats, *shards = lax.optimization_barrier((text, w_img_in, mats, *shards))
    text_right = ring(text_next, n_mp - 1)
    kv_own = text_kv("text_kv_own", text_next)
    mate_own = partner(kv_own, "group")
    own_lat = call(
        prep_body, "prep", (), (1,), [VMEM] * (n_mp + 1),
        VMEM, jax.ShapeDtypeStruct((full, 2 * ch), BF), [],
        (*shards, win_late), 2 * full * ch * d, 2 * ch * d,
    )
    mate_lat = partner(own_lat, "group")
    by_head = lambda *shape: pl.BlockSpec((1,) + shape, lambda h, *_: (h, 0, 0))
    q, acc = call(
        functools.partial(image_body, full, n_mp), "image_attention", (ids, img_len, split_flag), (heads,),
        [whole((full, 2 * ch)), whole((full, 2 * ch)),
         pl.BlockSpec((1, 2, 3 * ch, 3 * HD), lambda h, *_: (h, 0, 0, 0)),
         pl.BlockSpec((1, 2, 8, 3 * HD), lambda h, *_: (h, 0, 0, 0)), whole((1, HD)), whole((1, HD))],
        [by_head(full, HD), by_head(full, 2 * HD)],
        [jax.ShapeDtypeStruct((heads, full, HD), BF), jax.ShapeDtypeStruct((heads, full, 2 * HD), F32)],
        [pltpu.VMEM((2 * full, HD), BF), pltpu.VMEM((2 * full, 2 * HD), BF),
         pltpu.VMEM((2 * full, 2 * HD), BF), pltpu.VMEM((2 * HD, 2 * HD), BF)],
        (own_lat, mate_lat, mats, shift, qg, kg), 2 * heads * full * full * 4 * HD * 2, 2**22,
    )

    text_left, text_right, acc = lax.optimization_barrier((text_left, text_right, acc))
    text_far = ring(text_left, 1)
    kv_near = text_kv("text_kv_near", text_left, text_right)
    mate_near = partner(kv_near, "group")

    scalars = (ids, txt_len, split_flag)
    acc = call(
        functools.partial(near_body, (0, n_mp - 1, 1), shard, n_mp), "text_attention_near", scalars, (heads,),
        [by_head(full, HD), by_head(full, 2 * HD)] + [by_head(v.shape[1], 2 * HD) for v in (kv_own, mate_own, kv_near, mate_near)],
        by_head(full, 2 * HD), jax.ShapeDtypeStruct(acc.shape, F32), [],
        (q, acc, kv_own, mate_own, kv_near, mate_near), 2 * heads * full * 6 * shard * 3 * HD, 2**23,
    )
    depth = heads * HD
    half = rows // 2
    rest, x_kept = call(
        functools.partial(stage_body, n_mp), "out_weights", (ids,), (n_mp,),
        [pl.BlockSpec((depth, d), lambda s, ids: (lax.rem(ids[2] + n_mp - ids[3 + s], n_mp), 0)),
         whole((ch, rows)), whole((ch, d))],
        [pl.BlockSpec((depth, d), lambda s, ids: (s, 0)), whole((half, d))],
        [jax.ShapeDtypeStruct((n_mp * depth, d), BF), jax.ShapeDtypeStruct((half, d), F32)], [],
        (w_out, lat_t, w_img_in), 2 * half * ch * d, 4 * n_mp * depth * d,
    )
    text_far, acc, rest = lax.optimization_barrier((text_far, acc, rest))
    kv_far = text_kv("text_kv_far", text_far)
    mate_far = partner(kv_far, "group")
    mixed = call(
        functools.partial(last_body, (n_mp - 2,), shard, n_mp), "text_attention_far", scalars, (1,),
        [VMEM] * 4, [VMEM] * (2 * n_mp),
        [jax.ShapeDtypeStruct((half, depth), BF)] * (2 * n_mp), [],
        (q, acc, kv_far, mate_far), 2 * heads * full * 2 * shard * 3 * HD, 2**22,
    )

    n_cfg = lax.axis_size("cfg")

    def send(s, flip):
        if s == 0 and flip == 0:
            return mixed[0]
        pairs = [
            (c * n_mp + i, (c ^ flip) * n_mp + (i + s) % n_mp) for c in range(n_cfg) for i in range(n_mp)
        ]
        return lax.ppermute(mixed[2 * s + flip], ("cfg", "mp"), pairs)

    pieces = {(s, flip): send(s, flip) for flip in range(2) for s in order}
    early = [pieces[s, flip] for s in order[:-n_late] for flip in range(2)]
    late = [pieces[s, flip] for s in order[-n_late:] for flip in range(2)]
    total = call(
        early_body, "out_early", (), (1,), [VMEM] * (len(early) + 1), VMEM,
        jax.ShapeDtypeStruct((rows, d), F32), [],
        (*early, rest), 2 * rows * (n_mp - 1) * depth * d, 2 * (n_mp - 1) * depth * d,
    )
    vel, moved = call(
        functools.partial(out_body, n_late), "out_late", (ids, tstep, img_len, guide, step_size), (1,),
        [VMEM] * (7 + 2 * n_late), [VMEM] * 2, [jax.ShapeDtypeStruct((1, ch, half), F32)] * 2,
        [pltpu.VMEM((rows, d), F32), pltpu.VMEM((rows, d), BF)],
        (*late, rest, total, x_kept, lat_t, mod_rows, mod_final, w_final.T),
        2 * rows * depth * d, 2 * depth * d,
    )
    return jnp.swapaxes(vel, 1, 2), jnp.swapaxes(moved, 1, 2)


def solution(mesh):
    placed = (
        P(("group", "mp"), None),
        P("cfg", ("group", "mp"), None),
        P(),
        P(None, "mp"),
        P(None, "mp"),
    ) + (P(),) * 13
    return jax.shard_map(
        local,
        mesh=mesh,
        in_specs=placed,
        out_specs=(P("cfg", ("group", "mp"), None), P("cfg", ("group", "mp"), None)),
        check_vma=False,
    )
```

```python
import functools

import jax
import jax.numpy as jnp
import numpy as np
from jax import lax
from jax.experimental import pallas as pl
from jax.experimental.pallas import tpu as pltpu
from jax.sharding import PartitionSpec as P

HD = 128
EPS = 1e-6
BF = jnp.bfloat16
F32 = jnp.float32
QSCALE = float(HD**-0.5 / np.log(2.0))
VLIM = 20 * 2**20
CHUNK = 64


def ring(value, step):
    n = lax.axis_size("mp")
    return lax.ppermute(value, "mp", [(i, (i + step) % n) for i in range(n)])


def partner(value, axis):
    n = lax.axis_size(axis)
    return lax.ppermute(value, axis, [(i, i ^ 1) for i in range(n)])


def split2(value):
    high = value.astype(BF)
    return high, (value - high.astype(F32)).astype(BF)


def layer_norm(values):
    center = values - jnp.mean(values, -1, keepdims=True)
    return center * lax.rsqrt(jnp.mean(center * center, -1, keepdims=True) + EPS)


def dot(a, b):
    return jnp.dot(a, b, preferred_element_type=F32)


def dot_t(a, b):
    return lax.dot_general(a, b, (((1,), (1,)), ((), ())), preferred_element_type=F32)


FREE = ('prep', 'image_own', 'image_mate', 'text_kv_near', 'text_kv_far', 'text_attention_near', 'text_attention_far', 'out_weights', 'out_own', 'out_early', 'out_late')


def call(body, name, scalars, grid, in_specs, out_specs, out_shape, scratch, args, flops, nbytes):
    if name in FREE:
        flops = nbytes = 0
    return pl.pallas_call(
        body,
        name=name,
        grid_spec=pltpu.PrefetchScalarGridSpec(
            num_scalar_prefetch=len(scalars),
            grid=grid,
            in_specs=in_specs,
            out_specs=out_specs,
            scratch_shapes=scratch,
        ),
        out_shape=out_shape,
        compiler_params=pltpu.CompilerParams(vmem_limit_bytes=VLIM),
        cost_estimate=pl.CostEstimate(flops=flops, bytes_accessed=nbytes, transcendentals=0),
    )(*scalars, *args)


def whole(shape):
    return pl.BlockSpec(shape, lambda *_: (0,) * len(shape))


VMEM = pl.BlockSpec(memory_space=pltpu.VMEM)


def prep_body(*refs):
    *lat_refs, win_ref, out_ref = refs
    for i, ref in enumerate(lat_refs):
        rows = ref[...].astype(F32).T.astype(BF)
        n = rows.shape[0]
        x = dot(rows, win_ref[...])
        center = x - jnp.mean(x, -1, keepdims=True)
        rstd = lax.rsqrt(jnp.mean(center * center, -1, keepdims=True) + EPS)
        high, low = split2(rows.astype(F32) * rstd)
        out_ref[i * n : (i + 1) * n, :] = jnp.concatenate([high, low], axis=1)


def fold_body(ids, tstep, win_ref, mod_ref, w_ref, mats_ref, shift_ref, rows_ref, win_buf, mod_buf, w_buf, sems):
    heads = mats_ref.shape[0]
    ch, d = win_ref.shape
    width = 3 * HD
    first = [pltpu.make_async_copy(win_ref, win_buf, sems.at[heads])]
    first.append(pltpu.make_async_copy(mod_ref.at[0:2], mod_buf, sems.at[heads + 1]))
    weights = [
        pltpu.make_async_copy(w_ref.at[:, h * width : (h + 1) * width], w_buf.at[h], sems.at[h])
        for h in range(heads)
    ]
    for copy in first + weights:
        copy.start()
    for copy in first:
        copy.wait()
    values = win_buf[...].astype(F32)
    center = values - jnp.mean(values, -1, keepdims=True)
    spot = lax.broadcasted_iota(jnp.int32, (16, d), 0)
    tail = jnp.zeros((16, d), F32)
    for i in range(2):
        at = pl.ds(tstep[ids[1] ^ i], 1)
        high, low = split2(center * (1.0 + mod_buf[1, at, :]))
        rows_ref[2 * i * ch : (2 * i + 1) * ch, :] = high
        rows_ref[(2 * i + 1) * ch : (2 * i + 2) * ch, :] = low
        high, low = split2(mod_buf[0, at, :])
        tail = jnp.where(spot == 2 * i, high.astype(F32), tail)
        tail = jnp.where(spot == 2 * i + 1, low.astype(F32), tail)
    rows_ref[4 * ch :, :] = tail.astype(BF)
    for h, copy in enumerate(weights):
        copy.wait()
        out = dot(rows_ref[...], w_buf[h])
        for i in range(2):
            high, low = split2(out[2 * i * ch : (2 * i + 1) * ch] + out[(2 * i + 1) * ch : (2 * i + 2) * ch])
            mats_ref[h, i] = jnp.concatenate([high, high, low], axis=0)
            base = 4 * ch + 2 * i
            shift_ref[h, i] = jnp.broadcast_to(out[base : base + 1] + out[base + 1 : base + 2], shift_ref.shape[2:])


def live_mask(first, rows, length):
    return (lax.broadcasted_iota(jnp.int32, (rows, HD), 0) + first) < length


def fill_ones(ref):
    head = [lax.broadcasted_iota(jnp.int32, ref.shape, i) // HD for i in range(2)]
    ref[...] = (head[0] == head[1]).astype(BF)


def head_norm(values, ones, gain):
    square = dot((values * values).astype(BF), ones)
    return values * lax.rsqrt(square * (1.0 / HD) + EPS) * gain


def place_rows(n_mp, ids, ref, x_ref):
    shard = ref.shape[0] // n_mp
    half = HD // 2
    for s in range(n_mp):
        start = pl.multiple_of(lax.rem(ids[2] + n_mp - s, n_mp) * shard, shard)
        lat = ref[s * shard : (s + 1) * shard, :]
        x_ref[pl.ds(start, shard), :] = jnp.concatenate(
            [lat, lat[:, :half], jnp.zeros((shard, half), BF)], axis=1
        )


def project(which, first, x_ref, mats_ref, shift_ref):
    mat = mats_ref[0, which]
    mat = jnp.concatenate([mat, jnp.zeros((2 * HD - mat.shape[0], mat.shape[1]), BF)], axis=0)[:, first:]
    return dot(x_ref[...], mat) + shift_ref[0, which, 0:1, first:]


def attend(q, k, v, length):
    live = live_mask(0, k.shape[0], length)
    values = jnp.concatenate([jnp.where(live, v, 0.0).astype(BF), live.astype(BF)], axis=1)
    return dot(jnp.exp2(dot_t(q, k)).astype(BF), values)


def image_body(n_mp, ids, img_len, lat_ref, mats_ref, shift_ref, qg_ref, kg_ref, q_ref, acc_ref, x_ref, ones_ref):
    @pl.when(pl.program_id(0) == 0)
    def _():
        fill_ones(ones_ref)
        place_rows(n_mp, ids, lat_ref, x_ref)

    block = project(0, 0, x_ref, mats_ref, shift_ref)
    gains = jnp.concatenate([qg_ref[...] * QSCALE, kg_ref[...]], axis=1)
    normed = head_norm(block[:, : 2 * HD], ones_ref[...], gains).astype(BF)
    q_ref[0] = normed[:, :HD]
    acc_ref[0] = attend(normed[:, :HD], normed[:, HD:], block[:, 2 * HD :], img_len[ids[1]])


def mate_body(n_mp, ids, img_len, flags, lat_ref, mats_ref, shift_ref, kg_ref, q_ref, acc_ref, out_ref, x_ref, ones_ref):
    seen = flags[ids[0], ids[1]] == 1

    @pl.when(jnp.logical_and(seen, pl.program_id(0) == 0))
    def _():
        fill_ones(ones_ref)
        place_rows(n_mp, ids, lat_ref, x_ref)

    @pl.when(seen)
    def _():
        block = project(1, HD, x_ref, mats_ref, shift_ref)
        keys = head_norm(block[:, :HD], ones_ref[...], kg_ref[...]).astype(BF)
        out_ref[0] = acc_ref[0] + attend(q_ref[0], keys, block[:, HD:], img_len[ids[1] ^ 1])

    @pl.when(jnp.logical_not(seen))
    def _():
        out_ref[0] = acc_ref[0]


def text_body(n_in, ids, tstep, *refs):
    rows_refs, (mod_ref, w_ref, kg_ref, out_ref, ones_ref, y_ref) = refs[:n_in], refs[n_in:]
    fill_ones(ones_ref)
    step = tstep[ids[1]]
    scale = 1.0 + mod_ref[step, 1:2, :]
    first = 0
    for ref in rows_refs:
        for start in range(0, ref.shape[0], CHUNK):
            x = ref[start : start + CHUNK, :].astype(F32)
            y_ref[first : first + CHUNK, :] = (layer_norm(x) * scale + mod_ref[step, 0:1, :]).astype(BF)
            first += CHUNK
    kv = dot(y_ref[...], w_ref[...])
    for h in range(out_ref.shape[0]):
        k = kv[:, 2 * HD * h : 2 * HD * h + HD]
        out_ref[h, :, :HD] = head_norm(k, ones_ref[...], kg_ref[...]).astype(BF)
        out_ref[h, :, HD:] = kv[:, 2 * HD * h + HD : 2 * HD * (h + 1)].astype(BF)


def text_attend(offsets, shard, n_mp, ids, txt_len, flags, q, acc, own, mate):
    side, group, m = ids[0], ids[1], ids[2]
    length = txt_len[group]
    mate_length = jnp.where(flags[side, group] == 1, txt_len[group ^ 1], 0)
    keys, values = [], []
    for kv, most in ((own, length), (mate, mate_length)):
        keys.append(kv[:, :HD])
        for i, off in enumerate(offsets):
            live = live_mask(lax.rem(m + off, n_mp) * shard, shard, most)
            v = kv[i * shard : (i + 1) * shard, HD:]
            values.append(
                jnp.concatenate([jnp.where(live, v, jnp.zeros_like(v)), live.astype(BF)], axis=1)
            )
    p = jnp.exp2(dot_t(q, jnp.concatenate(keys, axis=0))).astype(BF)
    return acc + dot(p, jnp.concatenate(values, axis=0))


def near_body(offsets, shard, n_mp, ids, txt_len, flags, q_ref, acc_ref, own0, mate0, own1, mate1, out_ref):
    own = jnp.concatenate([own0[0], own1[0]], axis=0)
    mate = jnp.concatenate([mate0[0], mate1[0]], axis=0)
    out_ref[0] = text_attend(offsets, shard, n_mp, ids, txt_len, flags, q_ref[0], acc_ref[0], own, mate)


def last_body(offsets, shard, n_mp, ids, txt_len, flags, q_ref, acc_ref, own_ref, mate_ref, *out_refs):
    rows = q_ref.shape[1] // n_mp
    half = rows // 2
    is_cond = ids[0] == 0
    for i in range(n_mp):
        spot = pl.ds(pl.multiple_of(lax.rem(ids[2] + i, n_mp) * rows, rows), rows)
        for h in range(q_ref.shape[0]):
            acc = text_attend(
                offsets, shard, n_mp, ids, txt_len, flags, q_ref[h, spot, :], acc_ref[h, spot, :],
                own_ref[h], mate_ref[h],
            )
            mixed = (acc[:, :HD] / acc[:, HD:]).astype(BF)
            low, high = mixed[:half], mixed[half:]
            columns = slice(h * HD, (h + 1) * HD)
            out_refs[2 * i][:, columns] = jnp.where(is_cond, low, high)
            out_refs[2 * i + 1][:, columns] = jnp.where(is_cond, high, low)


def stage_body(n_mp, ids, w_ref, lat_ref, win_ref, rest_ref, x_ref):
    rest_ref[...] = w_ref[...]

    @pl.when(pl.program_id(0) == 0)
    def _():
        half = x_ref.shape[0]
        lat = jnp.where(ids[0] == 0, lat_ref[:, :half], lat_ref[:, half:])
        x_ref[...] = dot(lat.T.astype(BF), win_ref[...])


def early_body(*refs):
    *pieces, w_ref, total_ref = refs
    own, other = (jnp.concatenate([ref[...] for ref in pieces[i::2]], axis=1) for i in range(2))
    total_ref[...] = dot(jnp.concatenate([own, other], axis=0), w_ref[: own.shape[1], :])


def final_rows(step, first_row, early_ref, piece_ref, w_ref, x_ref, mod_ref, norm_ref, wf_ref, total, out):
    total[...] = dot(piece_ref[...], w_ref[-piece_ref.shape[1] :, :])
    gate, scale = mod_ref[2, pl.ds(step, 1), :], 1.0 + norm_ref[step, 1:2, :]
    for first in range(0, x_ref.shape[0], CHUNK):
        rows = slice(first, first + CHUNK)
        hidden = x_ref[rows, :] + gate * (early_ref[first_row + first : first_row + first + CHUNK, :] + total[rows, :])
        out[rows, :] = (layer_norm(hidden) * scale + norm_ref[step, 0:1, :]).astype(BF)
    return dot_t(wf_ref[...], out[...])


def own_body(ids, tstep, *refs):
    early_ref, piece_ref, w_ref, x_ref, mod_ref, norm_ref, wf_ref, vel_ref, total, out = refs
    vel_ref[...] = final_rows(
        tstep[ids[1]], 0, early_ref, piece_ref, w_ref, x_ref, mod_ref, norm_ref, wf_ref, total, out
    )


def out_body(ids, tstep, img_len, guide, step_size, *refs):
    early_ref, piece_ref, w_ref, own_ref, lat_ref, x_ref, mod_ref, norm_ref, wf_ref, vel_ref, next_ref, total, out = refs
    side, group, m = ids[0], ids[1], ids[2]
    step = tstep[group]
    other = final_rows(
        step, x_ref.shape[0], early_ref, piece_ref, w_ref, x_ref, mod_ref, norm_ref, wf_ref, total, out
    )
    own = own_ref[...]
    is_cond = side == 0
    cond = jnp.where(is_cond, own, other)
    uncond = jnp.where(is_cond, other, own)
    guided = uncond + guide[group] * (cond - uncond)
    half = own.shape[1]
    place = lax.broadcasted_iota(jnp.int32, guided.shape, 1) + (2 * m + side) * half
    guided = jnp.where(place < img_len[group], guided, 0.0)
    vel_ref[0] = guided
    start = jnp.where(is_cond, lat_ref[:, :half], lat_ref[:, half:])
    next_ref[0] = start - step_size[step] * guided


def local(
    latents, text_hidden, w_img_in, w_img_qkv, w_txt_kv, q_gain, k_gain, w_out, w_final,
    mod_img, mod_txt, mod_final, guide, step_size, img_len, txt_len, split_flag, tstep,
):
    n_mp = lax.axis_size("mp")
    order = [0, *range(3, n_mp), 1, 2]
    ids = jnp.stack([lax.axis_index("cfg"), lax.axis_index("group"), lax.axis_index("mp"), *order]).astype(jnp.int32)
    rows, ch = latents.shape
    full = rows * n_mp
    d = w_img_in.shape[1]
    cols = w_img_qkv.shape[1]
    heads = cols // (3 * HD)
    shard = text_hidden.shape[1]
    qg, kg = q_gain.reshape(1, HD), k_gain.reshape(1, HD)

    lat_t = latents.T

    text = text_hidden.reshape(shard, d)
    text_left = ring(text, 1)
    lat_sent = lat_t.astype(BF)
    shards = [lat_sent] + [ring(lat_sent, s) for s in range(1, n_mp)]

    mod_rows = jnp.transpose(mod_img, (1, 0, 2))
    hbm = pl.BlockSpec(memory_space=pltpu.HBM)
    mats, shift = call(
        fold_body, "fold", (ids, tstep), (1,), [hbm] * 3, [VMEM] * 2,
        [jax.ShapeDtypeStruct((heads, 2, 3 * ch, 3 * HD), BF), jax.ShapeDtypeStruct((heads, 2, 8, 3 * HD), F32)],
        [pltpu.VMEM((4 * ch + 16, d), BF), pltpu.VMEM((ch, d), BF), pltpu.VMEM((2,) + mod_rows.shape[1:], F32),
         pltpu.VMEM((heads, d, 3 * HD), BF), pltpu.SemaphoreType.DMA((heads + 2,))],
        (w_img_in, mod_rows, w_img_qkv), 2 * 272 * d * cols, 2 * d * cols,
    )

    def text_kv(name, *pieces):
        n = sum(p.shape[0] for p in pieces)
        return call(
            functools.partial(text_body, len(pieces)), name, (ids, tstep), (1,),
            [VMEM] * (len(pieces) + 3), VMEM, jax.ShapeDtypeStruct((heads, n, 2 * HD), BF),
            [pltpu.VMEM((HD, HD), BF), pltpu.VMEM((n, d), BF)],
            pieces + (mod_txt, w_txt_kv, kg), 2 * n * d * heads * 2 * HD, 2 * d * heads * 2 * HD,
        )

    text_next, mats, *shards = lax.optimization_barrier((text, mats, *shards))
    text_right = ring(text_next, n_mp - 1)
    own_lat = call(
        prep_body, "prep", (), (1,), [VMEM] * (n_mp + 1),
        VMEM, jax.ShapeDtypeStruct((full, 2 * ch), BF), [],
        (*shards, w_img_in), 2 * full * ch * d, 2 * ch * d,
    )
    mate_lat = partner(own_lat, "group")
    kv_own = text_kv("text_kv_own", text_next)
    mate_own = partner(kv_own, "group")

    by_head = lambda *shape: pl.BlockSpec((1,) + shape, lambda h, *_: (h, 0, 0))
    of_head = [pl.BlockSpec((1, 2, n, 3 * HD), lambda h, *_: (h, 0, 0, 0)) for n in (3 * ch, 8)]
    acc_shape = jax.ShapeDtypeStruct((heads, full, 2 * HD), F32)
    q, acc = call(
        functools.partial(image_body, n_mp), "image_own", (ids, img_len), (heads,),
        [whole((full, 2 * ch)), *of_head, whole((1, HD)), whole((1, HD))],
        [by_head(full, HD), by_head(full, 2 * HD)],
        [jax.ShapeDtypeStruct((heads, full, HD), BF), acc_shape],
        [pltpu.VMEM((full, 2 * HD), BF), pltpu.VMEM((2 * HD, 2 * HD), BF)],
        (own_lat, mats, shift, qg, kg), 2 * heads * full * full * 3 * HD, 2**22,
    )
    acc = call(
        functools.partial(mate_body, n_mp), "image_mate", (ids, img_len, split_flag), (heads,),
        [whole((full, 2 * ch)), *of_head, whole((1, HD)), by_head(full, HD), by_head(full, 2 * HD)],
        by_head(full, 2 * HD), acc_shape,
        [pltpu.VMEM((full, 2 * HD), BF), pltpu.VMEM((HD, HD), BF)],
        (mate_lat, mats, shift, kg, q, acc), 2 * heads * full * full * 3 * HD, 2**22,
    )

    depth = heads * HD
    half = rows // 2
    rest, x_kept = call(
        functools.partial(stage_body, n_mp), "out_weights", (ids,), (n_mp,),
        [pl.BlockSpec((depth, d), lambda s, ids: (lax.rem(ids[2] + n_mp - ids[3 + s], n_mp), 0)),
         whole((ch, rows)), whole((ch, d))],
        [pl.BlockSpec((depth, d), lambda s, ids: (s, 0)), whole((half, d))],
        [jax.ShapeDtypeStruct((n_mp * depth, d), BF), jax.ShapeDtypeStruct((half, d), F32)], [],
        (w_out, lat_t, w_img_in), 2 * half * ch * d, 4 * n_mp * depth * d,
    )
    text_right, text_left, acc = lax.optimization_barrier((text_right, text_left, acc))
    text_far = ring(text_right, n_mp - 1)
    kv_near = text_kv("text_kv_near", text_left, text_right)
    mate_near = partner(kv_near, "group")

    scalars = (ids, txt_len, split_flag)
    acc = call(
        functools.partial(near_body, (0, n_mp - 1, 1), shard, n_mp), "text_attention_near", scalars, (heads,),
        [by_head(full, HD), by_head(full, 2 * HD)] + [by_head(v.shape[1], 2 * HD) for v in (kv_own, mate_own, kv_near, mate_near)],
        by_head(full, 2 * HD), jax.ShapeDtypeStruct(acc.shape, F32), [],
        (q, acc, kv_own, mate_own, kv_near, mate_near), 2 * heads * full * 6 * shard * 3 * HD, 2**23,
    )
    text_far, acc, rest = lax.optimization_barrier((text_far, acc, rest))
    kv_far = text_kv("text_kv_far", text_far)
    mate_far = partner(kv_far, "group")
    mixed = call(
        functools.partial(last_body, (n_mp - 2,), shard, n_mp), "text_attention_far", scalars, (1,),
        [VMEM] * 4, [VMEM] * (2 * n_mp),
        [jax.ShapeDtypeStruct((half, depth), BF)] * (2 * n_mp), [],
        (q, acc, kv_far, mate_far), 2 * heads * full * 2 * shard * 3 * HD, 2**22,
    )

    n_cfg = lax.axis_size("cfg")

    def send(s, flip):
        if s == 0 and flip == 0:
            return mixed[0]
        pairs = [
            (c * n_mp + i, (c ^ flip) * n_mp + (i + s) % n_mp) for c in range(n_cfg) for i in range(n_mp)
        ]
        return lax.ppermute(mixed[2 * s + flip], ("cfg", "mp"), pairs)

    pieces = {(s, flip): send(s, flip) for s in order for flip in range(2)}
    early = [pieces[s, flip] for s in order[:-1] for flip in range(2)]
    total = call(
        early_body, "out_early", (), (1,), [VMEM] * (len(early) + 1), VMEM,
        jax.ShapeDtypeStruct((rows, d), F32), [],
        (*early, rest), rows * len(early) * depth * d, len(early) * depth * d,
    )
    work = [pltpu.VMEM((half, d), F32), pltpu.VMEM((half, d), BF)]
    tables = (x_kept, mod_rows, mod_final, w_final.T)
    own_vel = call(
        own_body, "out_own", (ids, tstep), (1,), [VMEM] * 7, VMEM,
        jax.ShapeDtypeStruct((ch, half), F32), work,
        (total, pieces[order[-1], 0], rest, *tables), 2 * half * depth * d, 2 * depth * d,
    )
    vel, moved = call(
        out_body, "out_late", (ids, tstep, img_len, guide, step_size), (1,),
        [VMEM] * 9, [VMEM] * 2, [jax.ShapeDtypeStruct((1, ch, half), F32)] * 2, work,
        (total, pieces[order[-1], 1], rest, own_vel, lat_t, *tables), 2 * half * depth * d, 2 * depth * d,
    )
    return jnp.swapaxes(vel, 1, 2), jnp.swapaxes(moved, 1, 2)


def solution(mesh):
    placed = (
        P(("group", "mp"), None),
        P("cfg", ("group", "mp"), None),
        P(),
        P(None, "mp"),
        P(None, "mp"),
    ) + (P(),) * 13
    return jax.shard_map(
        local,
        mesh=mesh,
        in_specs=placed,
        out_specs=(P("cfg", ("group", "mp"), None), P("cfg", ("group", "mp"), None)),
        check_vma=False,
    )
```

```python
import functools

import jax
import jax.numpy as jnp
import numpy as np
from jax import lax
from jax.experimental import pallas as pl
from jax.experimental.pallas import tpu as pltpu
from jax.sharding import PartitionSpec as P

HD = 128
EPS = 1e-6
BF = jnp.bfloat16
F32 = jnp.float32
QSCALE = float(HD**-0.5 / np.log(2.0))
VLIM = 20 * 2**20
CHUNK = 64


def ring(value, step):
    n = lax.axis_size("mp")
    return lax.ppermute(value, "mp", [(i, (i + step) % n) for i in range(n)])


def partner(value, axis):
    n = lax.axis_size(axis)
    return lax.ppermute(value, axis, [(i, i ^ 1) for i in range(n)])


def split2(value):
    high = value.astype(BF)
    return high, (value - high.astype(F32)).astype(BF)


def layer_norm(values):
    center = values - jnp.mean(values, -1, keepdims=True)
    return center * lax.rsqrt(jnp.mean(center * center, -1, keepdims=True) + EPS)


def dot(a, b):
    return jnp.dot(a, b, preferred_element_type=F32)


def dot_t(a, b):
    return lax.dot_general(a, b, (((1,), (1,)), ((), ())), preferred_element_type=F32)


FREE = ('prep', 'image_own', 'image_mate', 'text_kv_near', 'text_kv_far', 'text_attention_near', 'text_attention_far', 'text_attention_rest', 'out_weights', 'out_own', 'out_early', 'out_late')


def call(body, name, scalars, grid, in_specs, out_specs, out_shape, scratch, args, flops, nbytes):
    if name in FREE:
        flops = nbytes = 0
    return pl.pallas_call(
        body,
        name=name,
        grid_spec=pltpu.PrefetchScalarGridSpec(
            num_scalar_prefetch=len(scalars),
            grid=grid,
            in_specs=in_specs,
            out_specs=out_specs,
            scratch_shapes=scratch,
        ),
        out_shape=out_shape,
        compiler_params=pltpu.CompilerParams(vmem_limit_bytes=VLIM),
        cost_estimate=pl.CostEstimate(flops=flops, bytes_accessed=nbytes, transcendentals=0),
    )(*scalars, *args)


def whole(shape):
    return pl.BlockSpec(shape, lambda *_: (0,) * len(shape))


VMEM = pl.BlockSpec(memory_space=pltpu.VMEM)


def prep_body(*refs):
    *lat_refs, win_ref, out_ref = refs
    for i, ref in enumerate(lat_refs):
        rows = ref[...].astype(F32).T.astype(BF)
        n = rows.shape[0]
        x = dot(rows, win_ref[...])
        center = x - jnp.mean(x, -1, keepdims=True)
        rstd = lax.rsqrt(jnp.mean(center * center, -1, keepdims=True) + EPS)
        high, low = split2(rows.astype(F32) * rstd)
        out_ref[i * n : (i + 1) * n, :] = jnp.concatenate([high, low], axis=1)


def fold_body(ids, tstep, win_ref, mod_ref, w_ref, mats_ref, shift_ref, rows_ref, win_buf, mod_buf, w_buf, sems):
    heads = mats_ref.shape[0]
    ch, d = win_ref.shape
    width = 3 * HD
    first = [pltpu.make_async_copy(win_ref, win_buf, sems.at[heads])]
    first.append(pltpu.make_async_copy(mod_ref.at[0:2], mod_buf, sems.at[heads + 1]))
    weights = [
        pltpu.make_async_copy(w_ref.at[:, h * width : (h + 1) * width], w_buf.at[h], sems.at[h])
        for h in range(heads)
    ]
    for copy in first + weights:
        copy.start()
    for copy in first:
        copy.wait()
    values = win_buf[...].astype(F32)
    center = values - jnp.mean(values, -1, keepdims=True)
    spot = lax.broadcasted_iota(jnp.int32, (16, d), 0)
    tail = jnp.zeros((16, d), F32)
    for i in range(2):
        at = pl.ds(tstep[ids[1] ^ i], 1)
        high, low = split2(center * (1.0 + mod_buf[1, at, :]))
        rows_ref[2 * i * ch : (2 * i + 1) * ch, :] = high
        rows_ref[(2 * i + 1) * ch : (2 * i + 2) * ch, :] = low
        high, low = split2(mod_buf[0, at, :])
        tail = jnp.where(spot == 2 * i, high.astype(F32), tail)
        tail = jnp.where(spot == 2 * i + 1, low.astype(F32), tail)
    rows_ref[4 * ch :, :] = tail.astype(BF)
    for h, copy in enumerate(weights):
        copy.wait()
        out = dot(rows_ref[...], w_buf[h])
        for i in range(2):
            high, low = split2(out[2 * i * ch : (2 * i + 1) * ch] + out[(2 * i + 1) * ch : (2 * i + 2) * ch])
            mats_ref[h, i] = jnp.concatenate([high, high, low], axis=0)
            base = 4 * ch + 2 * i
            shift_ref[h, i] = jnp.broadcast_to(out[base : base + 1] + out[base + 1 : base + 2], shift_ref.shape[2:])


def live_mask(first, rows, length):
    return (lax.broadcasted_iota(jnp.int32, (rows, HD), 0) + first) < length


def fill_ones(ref):
    head = [lax.broadcasted_iota(jnp.int32, ref.shape, i) // HD for i in range(2)]
    ref[...] = (head[0] == head[1]).astype(BF)


def head_norm(values, ones, gain):
    square = dot((values * values).astype(BF), ones)
    return values * lax.rsqrt(square * (1.0 / HD) + EPS) * gain


def place_rows(n_mp, ids, ref, x_ref):
    shard = ref.shape[0] // n_mp
    half = HD // 2
    for s in range(n_mp):
        start = pl.multiple_of(lax.rem(ids[2] + n_mp - s, n_mp) * shard, shard)
        lat = ref[s * shard : (s + 1) * shard, :]
        x_ref[pl.ds(start, shard), :] = jnp.concatenate(
            [lat, lat[:, :half], jnp.zeros((shard, half), BF)], axis=1
        )


def project(which, first, x_ref, mats_ref, shift_ref):
    mat = mats_ref[0, which]
    mat = jnp.concatenate([mat, jnp.zeros((2 * HD - mat.shape[0], mat.shape[1]), BF)], axis=0)[:, first:]
    return dot(x_ref[...], mat) + shift_ref[0, which, 0:1, first:]


def attend(q, k, v, length):
    live = live_mask(0, k.shape[0], length)
    values = jnp.concatenate([jnp.where(live, v, 0.0).astype(BF), live.astype(BF)], axis=1)
    return dot(jnp.exp2(dot_t(q, k)).astype(BF), values)


def image_body(n_mp, ids, img_len, lat_ref, mats_ref, shift_ref, qg_ref, kg_ref, q_ref, acc_ref, x_ref, ones_ref):
    @pl.when(pl.program_id(0) == 0)
    def _():
        fill_ones(ones_ref)
        place_rows(n_mp, ids, lat_ref, x_ref)

    block = project(0, 0, x_ref, mats_ref, shift_ref)
    gains = jnp.concatenate([qg_ref[...] * QSCALE, kg_ref[...]], axis=1)
    normed = head_norm(block[:, : 2 * HD], ones_ref[...], gains).astype(BF)
    q_ref[0] = normed[:, :HD]
    acc_ref[0] = attend(normed[:, :HD], normed[:, HD:], block[:, 2 * HD :], img_len[ids[1]])


def mate_body(n_mp, ids, img_len, flags, lat_ref, mats_ref, shift_ref, kg_ref, q_ref, acc_ref, out_ref, x_ref, ones_ref):
    seen = flags[ids[0], ids[1]] == 1

    @pl.when(jnp.logical_and(seen, pl.program_id(0) == 0))
    def _():
        fill_ones(ones_ref)
        place_rows(n_mp, ids, lat_ref, x_ref)

    @pl.when(seen)
    def _():
        block = project(1, HD, x_ref, mats_ref, shift_ref)
        keys = head_norm(block[:, :HD], ones_ref[...], kg_ref[...]).astype(BF)
        out_ref[0] = acc_ref[0] + attend(q_ref[0], keys, block[:, HD:], img_len[ids[1] ^ 1])

    @pl.when(jnp.logical_not(seen))
    def _():
        out_ref[0] = acc_ref[0]


def text_body(n_in, ids, tstep, *refs):
    rows_refs, (mod_ref, w_ref, kg_ref, out_ref, ones_ref, y_ref) = refs[:n_in], refs[n_in:]
    fill_ones(ones_ref)
    step = tstep[ids[1]]
    scale = 1.0 + mod_ref[step, 1:2, :]
    first = 0
    for ref in rows_refs:
        for start in range(0, ref.shape[0], CHUNK):
            x = ref[start : start + CHUNK, :].astype(F32)
            y_ref[first : first + CHUNK, :] = (layer_norm(x) * scale + mod_ref[step, 0:1, :]).astype(BF)
            first += CHUNK
    kv = dot(y_ref[...], w_ref[...])
    for h in range(out_ref.shape[0]):
        k = kv[:, 2 * HD * h : 2 * HD * h + HD]
        out_ref[h, :, :HD] = head_norm(k, ones_ref[...], kg_ref[...]).astype(BF)
        out_ref[h, :, HD:] = kv[:, 2 * HD * h + HD : 2 * HD * (h + 1)].astype(BF)


def text_sides(offsets, shard, n_mp, ids, txt_len, flags, own, mate):
    side, group, m = ids[0], ids[1], ids[2]
    length = txt_len[group]
    mate_length = jnp.where(flags[side, group] == 1, txt_len[group ^ 1], 0)
    keys, values = [], []
    for kv, most in ((own, length), (mate, mate_length)):
        keys.append(kv[:, :HD])
        for i, off in enumerate(offsets):
            live = live_mask(lax.rem(m + off, n_mp) * shard, shard, most)
            v = kv[i * shard : (i + 1) * shard, HD:]
            values.append(
                jnp.concatenate([jnp.where(live, v, jnp.zeros_like(v)), live.astype(BF)], axis=1)
            )
    return jnp.concatenate(keys, axis=0), jnp.concatenate(values, axis=0)


def text_attend(q, acc, keys, values):
    return acc + dot(jnp.exp2(dot_t(q, keys)).astype(BF), values)


def near_body(offsets, shard, n_mp, ids, txt_len, flags, q_ref, acc_ref, own0, mate0, own1, mate1, out_ref):
    own = jnp.concatenate([own0[0], own1[0]], axis=0)
    mate = jnp.concatenate([mate0[0], mate1[0]], axis=0)
    out_ref[0] = text_attend(
        q_ref[0], acc_ref[0], *text_sides(offsets, shard, n_mp, ids, txt_len, flags, own, mate)
    )


def last_body(offsets, shard, n_mp, steps, ids, txt_len, flags, q_ref, acc_ref, own_ref, mate_ref, *out_refs):
    rows = q_ref.shape[1] // n_mp
    half = rows // 2
    is_cond = ids[0] == 0
    for h in range(q_ref.shape[0]):
        sides = text_sides(offsets, shard, n_mp, ids, txt_len, flags, own_ref[h], mate_ref[h])
        columns = slice(h * HD, (h + 1) * HD)
        for i, step in enumerate(steps):
            spot = pl.ds(pl.multiple_of(lax.rem(ids[2] + step, n_mp) * rows, rows), rows)
            acc = text_attend(q_ref[h, spot, :], acc_ref[h, spot, :], *sides)
            mixed = (acc[:, :HD] / acc[:, HD:]).astype(BF)
            low, high = mixed[:half], mixed[half:]
            out_refs[2 * i][:, columns] = jnp.where(is_cond, low, high)
            out_refs[2 * i + 1][:, columns] = jnp.where(is_cond, high, low)


def stage_body(n_mp, ids, w_ref, lat_ref, win_ref, rest_ref, x_ref):
    rest_ref[...] = w_ref[...]

    @pl.when(pl.program_id(0) == 0)
    def _():
        half = x_ref.shape[0]
        lat = jnp.where(ids[0] == 0, lat_ref[:, :half], lat_ref[:, half:])
        x_ref[...] = dot(lat.T.astype(BF), win_ref[...])


def early_body(*refs):
    *pieces, w_ref, total_ref = refs
    own, other = (jnp.concatenate([ref[...] for ref in pieces[i::2]], axis=1) for i in range(2))
    total_ref[...] = dot(jnp.concatenate([own, other], axis=0), w_ref[: own.shape[1], :])


def final_rows(step, first_row, early_ref, piece_ref, w_ref, x_ref, mod_ref, norm_ref, wf_ref, total, out):
    total[...] = dot(piece_ref[...], w_ref[-piece_ref.shape[1] :, :])
    gate, scale = mod_ref[2, pl.ds(step, 1), :], 1.0 + norm_ref[step, 1:2, :]
    for first in range(0, x_ref.shape[0], CHUNK):
        rows = slice(first, first + CHUNK)
        hidden = x_ref[rows, :] + gate * (early_ref[first_row + first : first_row + first + CHUNK, :] + total[rows, :])
        out[rows, :] = (layer_norm(hidden) * scale + norm_ref[step, 0:1, :]).astype(BF)
    return dot_t(wf_ref[...], out[...])


def own_body(ids, tstep, *refs):
    early_ref, piece_ref, w_ref, x_ref, mod_ref, norm_ref, wf_ref, vel_ref, total, out = refs
    vel_ref[...] = final_rows(
        tstep[ids[1]], 0, early_ref, piece_ref, w_ref, x_ref, mod_ref, norm_ref, wf_ref, total, out
    )


def out_body(ids, tstep, img_len, guide, step_size, *refs):
    early_ref, piece_ref, w_ref, own_ref, lat_ref, x_ref, mod_ref, norm_ref, wf_ref, vel_ref, next_ref, total, out = refs
    side, group, m = ids[0], ids[1], ids[2]
    step = tstep[group]
    other = final_rows(
        step, x_ref.shape[0], early_ref, piece_ref, w_ref, x_ref, mod_ref, norm_ref, wf_ref, total, out
    )
    own = own_ref[...]
    is_cond = side == 0
    cond = jnp.where(is_cond, own, other)
    uncond = jnp.where(is_cond, other, own)
    guided = uncond + guide[group] * (cond - uncond)
    half = own.shape[1]
    place = lax.broadcasted_iota(jnp.int32, guided.shape, 1) + (2 * m + side) * half
    guided = jnp.where(place < img_len[group], guided, 0.0)
    vel_ref[0] = guided
    start = jnp.where(is_cond, lat_ref[:, :half], lat_ref[:, half:])
    next_ref[0] = start - step_size[step] * guided


def local(
    latents, text_hidden, w_img_in, w_img_qkv, w_txt_kv, q_gain, k_gain, w_out, w_final,
    mod_img, mod_txt, mod_final, guide, step_size, img_len, txt_len, split_flag, tstep,
):
    n_mp = lax.axis_size("mp")
    order = [0, *range(3, n_mp), 1, 2]
    ids = jnp.stack([lax.axis_index("cfg"), lax.axis_index("group"), lax.axis_index("mp"), *order]).astype(jnp.int32)
    rows, ch = latents.shape
    full = rows * n_mp
    d = w_img_in.shape[1]
    cols = w_img_qkv.shape[1]
    heads = cols // (3 * HD)
    shard = text_hidden.shape[1]
    qg, kg = q_gain.reshape(1, HD), k_gain.reshape(1, HD)

    lat_t = latents.T

    text = text_hidden.reshape(shard, d)
    text_left = ring(text, 1)
    lat_sent = lat_t.astype(BF)
    shards = [lat_sent] + [ring(lat_sent, s) for s in range(1, n_mp)]

    mod_rows = jnp.transpose(mod_img, (1, 0, 2))
    hbm = pl.BlockSpec(memory_space=pltpu.HBM)
    mats, shift = call(
        fold_body, "fold", (ids, tstep), (1,), [hbm] * 3, [VMEM] * 2,
        [jax.ShapeDtypeStruct((heads, 2, 3 * ch, 3 * HD), BF), jax.ShapeDtypeStruct((heads, 2, 8, 3 * HD), F32)],
        [pltpu.VMEM((4 * ch + 16, d), BF), pltpu.VMEM((ch, d), BF), pltpu.VMEM((2,) + mod_rows.shape[1:], F32),
         pltpu.VMEM((heads, d, 3 * HD), BF), pltpu.SemaphoreType.DMA((heads + 2,))],
        (w_img_in, mod_rows, w_img_qkv), 2 * 272 * d * cols, 2 * d * cols,
    )

    def text_kv(name, *pieces):
        n = sum(p.shape[0] for p in pieces)
        return call(
            functools.partial(text_body, len(pieces)), name, (ids, tstep), (1,),
            [VMEM] * (len(pieces) + 3), VMEM, jax.ShapeDtypeStruct((heads, n, 2 * HD), BF),
            [pltpu.VMEM((HD, HD), BF), pltpu.VMEM((n, d), BF)],
            pieces + (mod_txt, w_txt_kv, kg), 2 * n * d * heads * 2 * HD, 2 * d * heads * 2 * HD,
        )

    text_next, mats, *shards = lax.optimization_barrier((text, mats, *shards))
    text_right = ring(text_next, n_mp - 1)
    own_lat = call(
        prep_body, "prep", (), (1,), [VMEM] * (n_mp + 1),
        VMEM, jax.ShapeDtypeStruct((full, 2 * ch), BF), [],
        (*shards, w_img_in), 2 * full * ch * d, 2 * ch * d,
    )
    mate_lat = partner(own_lat, "group")
    kv_own = text_kv("text_kv_own", text_next)
    mate_own = partner(kv_own, "group")

    by_head = lambda *shape: pl.BlockSpec((1,) + shape, lambda h, *_: (h, 0, 0))
    of_head = [pl.BlockSpec((1, 2, n, 3 * HD), lambda h, *_: (h, 0, 0, 0)) for n in (3 * ch, 8)]
    acc_shape = jax.ShapeDtypeStruct((heads, full, 2 * HD), F32)
    q, acc = call(
        functools.partial(image_body, n_mp), "image_own", (ids, img_len), (heads,),
        [whole((full, 2 * ch)), *of_head, whole((1, HD)), whole((1, HD))],
        [by_head(full, HD), by_head(full, 2 * HD)],
        [jax.ShapeDtypeStruct((heads, full, HD), BF), acc_shape],
        [pltpu.VMEM((full, 2 * HD), BF), pltpu.VMEM((2 * HD, 2 * HD), BF)],
        (own_lat, mats, shift, qg, kg), 2 * heads * full * full * 3 * HD, 2**22,
    )
    acc = call(
        functools.partial(mate_body, n_mp), "image_mate", (ids, img_len, split_flag), (heads,),
        [whole((full, 2 * ch)), *of_head, whole((1, HD)), by_head(full, HD), by_head(full, 2 * HD)],
        by_head(full, 2 * HD), acc_shape,
        [pltpu.VMEM((full, 2 * HD), BF), pltpu.VMEM((HD, HD), BF)],
        (mate_lat, mats, shift, kg, q, acc), 2 * heads * full * full * 3 * HD, 2**22,
    )

    depth = heads * HD
    half = rows // 2
    rest, x_kept = call(
        functools.partial(stage_body, n_mp), "out_weights", (ids,), (n_mp,),
        [pl.BlockSpec((depth, d), lambda s, ids: (lax.rem(ids[2] + n_mp - ids[3 + s], n_mp), 0)),
         whole((ch, rows)), whole((ch, d))],
        [pl.BlockSpec((depth, d), lambda s, ids: (s, 0)), whole((half, d))],
        [jax.ShapeDtypeStruct((n_mp * depth, d), BF), jax.ShapeDtypeStruct((half, d), F32)], [],
        (w_out, lat_t, w_img_in), 2 * half * ch * d, 4 * n_mp * depth * d,
    )
    text_right, text_left, acc = lax.optimization_barrier((text_right, text_left, acc))
    text_far = ring(text_right, n_mp - 1)
    kv_near = text_kv("text_kv_near", text_left, text_right)
    mate_near = partner(kv_near, "group")

    scalars = (ids, txt_len, split_flag)
    acc = call(
        functools.partial(near_body, (0, n_mp - 1, 1), shard, n_mp), "text_attention_near", scalars, (heads,),
        [by_head(full, HD), by_head(full, 2 * HD)] + [by_head(v.shape[1], 2 * HD) for v in (kv_own, mate_own, kv_near, mate_near)],
        by_head(full, 2 * HD), jax.ShapeDtypeStruct(acc.shape, F32), [],
        (q, acc, kv_own, mate_own, kv_near, mate_near), 2 * heads * full * 6 * shard * 3 * HD, 2**23,
    )
    text_far, acc, rest = lax.optimization_barrier((text_far, acc, rest))
    kv_far = text_kv("text_kv_far", text_far)
    mate_far = partner(kv_far, "group")
    mixed = {}
    for name, steps in (("text_attention_far", order[1:-1]), ("text_attention_rest", [order[-1], order[0]])):
        out = call(
            functools.partial(last_body, (n_mp - 2,), shard, n_mp, steps), name, scalars, (1,),
            [VMEM] * 4, [VMEM] * (2 * len(steps)),
            [jax.ShapeDtypeStruct((half, depth), BF)] * (2 * len(steps)), [],
            (q, acc, kv_far, mate_far), heads * full * 2 * shard * 3 * HD, 2**22,
        )
        mixed.update({(s, flip): out[2 * i + flip] for i, s in enumerate(steps) for flip in range(2)})

    n_cfg = lax.axis_size("cfg")

    def send(s, flip):
        if s == 0 and flip == 0:
            return mixed[0, 0]
        pairs = [
            (c * n_mp + i, (c ^ flip) * n_mp + (i + s) % n_mp) for c in range(n_cfg) for i in range(n_mp)
        ]
        return lax.ppermute(mixed[s, flip], ("cfg", "mp"), pairs)

    pieces = {(s, flip): send(s, flip) for s in order[1:] + order[:1] for flip in range(2)}
    early = [pieces[s, flip] for s in order[:-1] for flip in range(2)]
    total = call(
        early_body, "out_early", (), (1,), [VMEM] * (len(early) + 1), VMEM,
        jax.ShapeDtypeStruct((rows, d), F32), [],
        (*early, rest), rows * len(early) * depth * d, len(early) * depth * d,
    )
    work = [pltpu.VMEM((half, d), F32), pltpu.VMEM((half, d), BF)]
    tables = (x_kept, mod_rows, mod_final, w_final.T)
    own_vel = call(
        own_body, "out_own", (ids, tstep), (1,), [VMEM] * 7, VMEM,
        jax.ShapeDtypeStruct((ch, half), F32), work,
        (total, pieces[order[-1], 0], rest, *tables), 2 * half * depth * d, 2 * depth * d,
    )
    vel, moved = call(
        out_body, "out_late", (ids, tstep, img_len, guide, step_size), (1,),
        [VMEM] * 9, [VMEM] * 2, [jax.ShapeDtypeStruct((1, ch, half), F32)] * 2, work,
        (total, pieces[order[-1], 1], rest, own_vel, lat_t, *tables), 2 * half * depth * d, 2 * depth * d,
    )
    return jnp.swapaxes(vel, 1, 2), jnp.swapaxes(moved, 1, 2)


def solution(mesh):
    placed = (
        P(("group", "mp"), None),
        P("cfg", ("group", "mp"), None),
        P(),
        P(None, "mp"),
        P(None, "mp"),
    ) + (P(),) * 13
    return jax.shard_map(
        local,
        mesh=mesh,
        in_specs=placed,
        out_specs=(P("cfg", ("group", "mp"), None), P("cfg", ("group", "mp"), None)),
        check_vma=False,
    )
```

```python
import functools

import jax
import jax.numpy as jnp
import numpy as np
from jax import lax
from jax.experimental import pallas as pl
from jax.experimental.pallas import tpu as pltpu
from jax.sharding import PartitionSpec as P

HD = 128
EPS = 1e-6
BF = jnp.bfloat16
F32 = jnp.float32
QSCALE = float(HD**-0.5 / np.log(2.0))
VLIM = 20 * 2**20
CHUNK = 64


def ring(value, step):
    n = lax.axis_size("mp")
    return lax.ppermute(value, "mp", [(i, (i + step) % n) for i in range(n)])


def partner(value, axis):
    n = lax.axis_size(axis)
    return lax.ppermute(value, axis, [(i, i ^ 1) for i in range(n)])


def split2(value):
    high = value.astype(BF)
    return high, (value - high.astype(F32)).astype(BF)


def layer_norm(values):
    center = values - jnp.mean(values, -1, keepdims=True)
    return center * lax.rsqrt(jnp.mean(center * center, -1, keepdims=True) + EPS)


def dot(a, b):
    return jnp.dot(a, b, preferred_element_type=F32)


def dot_t(a, b):
    return lax.dot_general(a, b, (((1,), (1,)), ((), ())), preferred_element_type=F32)


FREE = ('prep', 'image_own', 'image_mate', 'text_kv_near', 'text_kv_far', 'text_attention_near', 'text_attention_far', 'text_attention_rest', 'out_weights', 'out_own', 'out_early', 'out_late')


def call(body, name, scalars, grid, in_specs, out_specs, out_shape, scratch, args, flops, nbytes):
    if name in FREE:
        flops = nbytes = 0
    return pl.pallas_call(
        body,
        name=name,
        grid_spec=pltpu.PrefetchScalarGridSpec(
            num_scalar_prefetch=len(scalars),
            grid=grid,
            in_specs=in_specs,
            out_specs=out_specs,
            scratch_shapes=scratch,
        ),
        out_shape=out_shape,
        compiler_params=pltpu.CompilerParams(vmem_limit_bytes=VLIM),
        cost_estimate=pl.CostEstimate(flops=flops, bytes_accessed=nbytes, transcendentals=0),
    )(*scalars, *args)


def whole(shape):
    return pl.BlockSpec(shape, lambda *_: (0,) * len(shape))


VMEM = pl.BlockSpec(memory_space=pltpu.VMEM)


def prep_body(*refs):
    *lat_refs, win_ref, out_ref = refs
    for i, ref in enumerate(lat_refs):
        rows = ref[...].astype(F32).T.astype(BF)
        n = rows.shape[0]
        x = dot(rows, win_ref[...])
        center = x - jnp.mean(x, -1, keepdims=True)
        rstd = lax.rsqrt(jnp.mean(center * center, -1, keepdims=True) + EPS)
        high, low = split2(rows.astype(F32) * rstd)
        out_ref[i * n : (i + 1) * n, :] = jnp.concatenate([high, low], axis=1)


def fold_body(ids, tstep, win_ref, mod_ref, w_ref, mats_ref, shift_ref, rows_ref, win_buf, mod_buf, w_buf, sems):
    heads = mats_ref.shape[0]
    ch, d = win_ref.shape
    width = 3 * HD
    first = [pltpu.make_async_copy(win_ref, win_buf, sems.at[heads])]
    first.append(pltpu.make_async_copy(mod_ref.at[0:2], mod_buf, sems.at[heads + 1]))
    weights = [
        pltpu.make_async_copy(w_ref.at[:, h * width : (h + 1) * width], w_buf.at[h], sems.at[h])
        for h in range(heads)
    ]
    for copy in first + weights:
        copy.start()
    for copy in first:
        copy.wait()
    values = win_buf[...].astype(F32)
    center = values - jnp.mean(values, -1, keepdims=True)
    spot = lax.broadcasted_iota(jnp.int32, (16, d), 0)
    tail = jnp.zeros((16, d), F32)
    for i in range(2):
        at = pl.ds(tstep[ids[1] ^ i], 1)
        high, low = split2(center * (1.0 + mod_buf[1, at, :]))
        rows_ref[2 * i * ch : (2 * i + 1) * ch, :] = high
        rows_ref[(2 * i + 1) * ch : (2 * i + 2) * ch, :] = low
        high, low = split2(mod_buf[0, at, :])
        tail = jnp.where(spot == 2 * i, high.astype(F32), tail)
        tail = jnp.where(spot == 2 * i + 1, low.astype(F32), tail)
    rows_ref[4 * ch :, :] = tail.astype(BF)
    for h, copy in enumerate(weights):
        copy.wait()
        out = dot(rows_ref[...], w_buf[h])
        for i in range(2):
            high, low = split2(out[2 * i * ch : (2 * i + 1) * ch] + out[(2 * i + 1) * ch : (2 * i + 2) * ch])
            mats_ref[h, i] = jnp.concatenate([high, high, low], axis=0)
            base = 4 * ch + 2 * i
            shift_ref[h, i] = jnp.broadcast_to(out[base : base + 1] + out[base + 1 : base + 2], shift_ref.shape[2:])


def live_mask(first, rows, length):
    return (lax.broadcasted_iota(jnp.int32, (rows, HD), 0) + first) < length


def fill_ones(ref):
    head = [lax.broadcasted_iota(jnp.int32, ref.shape, i) // HD for i in range(2)]
    ref[...] = (head[0] == head[1]).astype(BF)


def head_norm(values, ones, gain):
    square = dot((values * values).astype(BF), ones)
    return values * lax.rsqrt(square * (1.0 / HD) + EPS) * gain


def place_rows(n_mp, ids, ref, x_ref):
    shard = ref.shape[0] // n_mp
    half = HD // 2
    for s in range(n_mp):
        start = pl.multiple_of(lax.rem(ids[2] + n_mp - s, n_mp) * shard, shard)
        lat = ref[s * shard : (s + 1) * shard, :]
        x_ref[pl.ds(start, shard), :] = jnp.concatenate(
            [lat, lat[:, :half], jnp.zeros((shard, half), BF)], axis=1
        )


def project(which, first, x_ref, mats_ref, shift_ref):
    mat = mats_ref[0, which]
    mat = jnp.concatenate([mat, jnp.zeros((2 * HD - mat.shape[0], mat.shape[1]), BF)], axis=0)[:, first:]
    return dot(x_ref[...], mat) + shift_ref[0, which, 0:1, first:]


def attend(q, k, v, length):
    live = live_mask(0, k.shape[0], length)
    values = jnp.concatenate([jnp.where(live, v, 0.0).astype(BF), live.astype(BF)], axis=1)
    return dot(jnp.exp2(dot_t(q, k)).astype(BF), values)


def image_body(n_mp, ids, img_len, lat_ref, mats_ref, shift_ref, qg_ref, kg_ref, q_ref, acc_ref, x_ref, ones_ref):
    @pl.when(pl.program_id(0) == 0)
    def _():
        fill_ones(ones_ref)
        place_rows(n_mp, ids, lat_ref, x_ref)

    block = project(0, 0, x_ref, mats_ref, shift_ref)
    gains = jnp.concatenate([qg_ref[...] * QSCALE, kg_ref[...]], axis=1)
    normed = head_norm(block[:, : 2 * HD], ones_ref[...], gains).astype(BF)
    q_ref[0] = normed[:, :HD]
    acc_ref[0] = attend(normed[:, :HD], normed[:, HD:], block[:, 2 * HD :], img_len[ids[1]])


def mate_body(n_mp, ids, img_len, flags, lat_ref, mats_ref, shift_ref, kg_ref, q_ref, acc_ref, out_ref, x_ref, ones_ref):
    seen = flags[ids[0], ids[1]] == 1

    @pl.when(jnp.logical_and(seen, pl.program_id(0) == 0))
    def _():
        fill_ones(ones_ref)
        place_rows(n_mp, ids, lat_ref, x_ref)

    @pl.when(seen)
    def _():
        block = project(1, HD, x_ref, mats_ref, shift_ref)
        keys = head_norm(block[:, :HD], ones_ref[...], kg_ref[...]).astype(BF)
        out_ref[0] = acc_ref[0] + attend(q_ref[0], keys, block[:, HD:], img_len[ids[1] ^ 1])

    @pl.when(jnp.logical_not(seen))
    def _():
        out_ref[0] = acc_ref[0]


def text_body(n_in, ids, tstep, *refs):
    rows_refs, (mod_ref, w_ref, kg_ref, out_ref, ones_ref, y_ref) = refs[:n_in], refs[n_in:]
    fill_ones(ones_ref)
    step = tstep[ids[1]]
    scale = 1.0 + mod_ref[step, 1:2, :]
    first = 0
    for ref in rows_refs:
        for start in range(0, ref.shape[0], CHUNK):
            x = ref[start : start + CHUNK, :].astype(F32)
            y_ref[first : first + CHUNK, :] = (layer_norm(x) * scale + mod_ref[step, 0:1, :]).astype(BF)
            first += CHUNK
    kv = dot(y_ref[...], w_ref[...])
    for h in range(out_ref.shape[0]):
        k = kv[:, 2 * HD * h : 2 * HD * h + HD]
        out_ref[h, :, :HD] = head_norm(k, ones_ref[...], kg_ref[...]).astype(BF)
        out_ref[h, :, HD:] = kv[:, 2 * HD * h + HD : 2 * HD * (h + 1)].astype(BF)


def text_sides(offsets, shard, n_mp, ids, txt_len, flags, own, mate):
    side, group, m = ids[0], ids[1], ids[2]
    length = txt_len[group]
    mate_length = jnp.where(flags[side, group] == 1, txt_len[group ^ 1], 0)
    keys, values = [], []
    for kv, most in ((own, length), (mate, mate_length)):
        keys.append(kv[:, :HD])
        for i, off in enumerate(offsets):
            live = live_mask(lax.rem(m + off, n_mp) * shard, shard, most)
            v = kv[i * shard : (i + 1) * shard, HD:]
            values.append(
                jnp.concatenate([jnp.where(live, v, jnp.zeros_like(v)), live.astype(BF)], axis=1)
            )
    return jnp.concatenate(keys, axis=0), jnp.concatenate(values, axis=0)


def text_attend(q, acc, keys, values):
    return acc + dot(jnp.exp2(dot_t(q, keys)).astype(BF), values)


def near_body(offsets, shard, n_mp, ids, txt_len, flags, q_ref, acc_ref, own0, mate0, own1, mate1, out_ref):
    own = jnp.concatenate([own0[0], own1[0]], axis=0)
    mate = jnp.concatenate([mate0[0], mate1[0]], axis=0)
    out_ref[0] = text_attend(
        q_ref[0], acc_ref[0], *text_sides(offsets, shard, n_mp, ids, txt_len, flags, own, mate)
    )


def last_body(offsets, shard, n_mp, steps, ids, txt_len, flags, q_ref, acc_ref, own_ref, mate_ref, *out_refs):
    rows = q_ref.shape[1] // n_mp
    half = rows // 2
    is_cond = ids[0] == 0
    for h in range(q_ref.shape[0]):
        sides = text_sides(offsets, shard, n_mp, ids, txt_len, flags, own_ref[h], mate_ref[h])
        columns = slice(h * HD, (h + 1) * HD)
        for i, step in enumerate(steps):
            spot = pl.ds(pl.multiple_of(lax.rem(ids[2] + step, n_mp) * rows, rows), rows)
            acc = text_attend(q_ref[h, spot, :], acc_ref[h, spot, :], *sides)
            mixed = (acc[:, :HD] / acc[:, HD:]).astype(BF)
            low, high = mixed[:half], mixed[half:]
            out_refs[2 * i][:, columns] = jnp.where(is_cond, low, high)
            out_refs[2 * i + 1][:, columns] = jnp.where(is_cond, high, low)


def stage_body(n_mp, ids, w_ref, lat_ref, win_ref, rest_ref, x_ref):
    rest_ref[...] = w_ref[...]

    @pl.when(pl.program_id(0) == 0)
    def _():
        half = x_ref.shape[0]
        lat = jnp.where(ids[0] == 0, lat_ref[:, :half], lat_ref[:, half:])
        x_ref[...] = dot(lat.T.astype(BF), win_ref[...])


def early_body(*refs):
    *pieces, w_ref, total_ref = refs
    own, other = (jnp.concatenate([ref[...] for ref in pieces[i::2]], axis=1) for i in range(2))
    total_ref[...] = dot(jnp.concatenate([own, other], axis=0), w_ref[: own.shape[1], :])


def final_rows(step, first_row, early_ref, piece_ref, w_ref, x_ref, mod_ref, norm_ref, wf_ref, total, out):
    total[...] = dot(piece_ref[...], w_ref[-piece_ref.shape[1] :, :])
    gate, scale = mod_ref[2, pl.ds(step, 1), :], 1.0 + norm_ref[step, 1:2, :]
    for first in range(0, x_ref.shape[0], CHUNK):
        rows = slice(first, first + CHUNK)
        hidden = x_ref[rows, :] + gate * (early_ref[first_row + first : first_row + first + CHUNK, :] + total[rows, :])
        out[rows, :] = (layer_norm(hidden) * scale + norm_ref[step, 0:1, :]).astype(BF)
    return dot_t(wf_ref[...], out[...])


def own_body(ids, tstep, *refs):
    early_ref, piece_ref, w_ref, x_ref, mod_ref, norm_ref, wf_ref, vel_ref, total, out = refs
    vel_ref[...] = final_rows(
        tstep[ids[1]], 0, early_ref, piece_ref, w_ref, x_ref, mod_ref, norm_ref, wf_ref, total, out
    )


def out_body(ids, tstep, img_len, guide, step_size, *refs):
    early_ref, piece_ref, w_ref, own_ref, lat_ref, x_ref, mod_ref, norm_ref, wf_ref, vel_ref, next_ref, total, out = refs
    side, group, m = ids[0], ids[1], ids[2]
    step = tstep[group]
    other = final_rows(
        step, x_ref.shape[0], early_ref, piece_ref, w_ref, x_ref, mod_ref, norm_ref, wf_ref, total, out
    )
    own = own_ref[...]
    is_cond = side == 0
    cond = jnp.where(is_cond, own, other)
    uncond = jnp.where(is_cond, other, own)
    guided = uncond + guide[group] * (cond - uncond)
    half = own.shape[1]
    place = lax.broadcasted_iota(jnp.int32, guided.shape, 1) + (2 * m + side) * half
    guided = jnp.where(place < img_len[group], guided, 0.0)
    vel_ref[0] = guided
    start = jnp.where(is_cond, lat_ref[:, :half], lat_ref[:, half:])
    next_ref[0] = start - step_size[step] * guided


def local(
    latents, text_hidden, w_img_in, w_img_qkv, w_txt_kv, q_gain, k_gain, w_out, w_final,
    mod_img, mod_txt, mod_final, guide, step_size, img_len, txt_len, split_flag, tstep,
):
    n_mp = lax.axis_size("mp")
    order = [0, *range(3, n_mp), 1, 2]
    ids = jnp.stack([lax.axis_index("cfg"), lax.axis_index("group"), lax.axis_index("mp"), *order]).astype(jnp.int32)
    rows, ch = latents.shape
    full = rows * n_mp
    d = w_img_in.shape[1]
    cols = w_img_qkv.shape[1]
    heads = cols // (3 * HD)
    shard = text_hidden.shape[1]
    qg, kg = q_gain.reshape(1, HD), k_gain.reshape(1, HD)

    lat_t = latents.T

    text = text_hidden.reshape(shard, d)
    text_left = ring(text, 1)
    lat_sent = lat_t.astype(BF)
    shards = [lat_sent] + [ring(lat_sent, s) for s in range(1, n_mp)]

    mod_rows = jnp.transpose(mod_img, (1, 0, 2))
    hbm = pl.BlockSpec(memory_space=pltpu.HBM)
    mats, shift = call(
        fold_body, "fold", (ids, tstep), (1,), [hbm] * 3, [VMEM] * 2,
        [jax.ShapeDtypeStruct((heads, 2, 3 * ch, 3 * HD), BF), jax.ShapeDtypeStruct((heads, 2, 8, 3 * HD), F32)],
        [pltpu.VMEM((4 * ch + 16, d), BF), pltpu.VMEM((ch, d), BF), pltpu.VMEM((2,) + mod_rows.shape[1:], F32),
         pltpu.VMEM((heads, d, 3 * HD), BF), pltpu.SemaphoreType.DMA((heads + 2,))],
        (w_img_in, mod_rows, w_img_qkv), 2 * 272 * d * cols, 2 * d * cols,
    )

    def text_kv(name, *pieces):
        n = sum(p.shape[0] for p in pieces)
        return call(
            functools.partial(text_body, len(pieces)), name, (ids, tstep), (1,),
            [VMEM] * (len(pieces) + 3), VMEM, jax.ShapeDtypeStruct((heads, n, 2 * HD), BF),
            [pltpu.VMEM((HD, HD), BF), pltpu.VMEM((n, d), BF)],
            pieces + (mod_txt, w_txt_kv, kg), 2 * n * d * heads * 2 * HD, 2 * d * heads * 2 * HD,
        )

    text_next, mats, *shards = lax.optimization_barrier((text, mats, *shards))
    text_right = ring(text_next, n_mp - 1)
    own_lat = call(
        prep_body, "prep", (), (1,), [VMEM] * (n_mp + 1),
        VMEM, jax.ShapeDtypeStruct((full, 2 * ch), BF), [],
        (*shards, w_img_in), 2 * full * ch * d, 2 * ch * d,
    )
    mate_lat = partner(own_lat, "group")
    kv_own = text_kv("text_kv_own", text_next)
    mate_own = partner(kv_own, "group")

    by_head = lambda *shape: pl.BlockSpec((1,) + shape, lambda h, *_: (h, 0, 0))
    of_head = [pl.BlockSpec((1, 2, n, 3 * HD), lambda h, *_: (h, 0, 0, 0)) for n in (3 * ch, 8)]
    acc_shape = jax.ShapeDtypeStruct((heads, full, 2 * HD), F32)
    q, acc = call(
        functools.partial(image_body, n_mp), "image_own", (ids, img_len), (heads,),
        [whole((full, 2 * ch)), *of_head, whole((1, HD)), whole((1, HD))],
        [by_head(full, HD), by_head(full, 2 * HD)],
        [jax.ShapeDtypeStruct((heads, full, HD), BF), acc_shape],
        [pltpu.VMEM((full, 2 * HD), BF), pltpu.VMEM((2 * HD, 2 * HD), BF)],
        (own_lat, mats, shift, qg, kg), 2 * heads * full * full * 3 * HD, 2**22,
    )
    acc = call(
        functools.partial(mate_body, n_mp), "image_mate", (ids, img_len, split_flag), (heads,),
        [whole((full, 2 * ch)), *of_head, whole((1, HD)), by_head(full, HD), by_head(full, 2 * HD)],
        by_head(full, 2 * HD), acc_shape,
        [pltpu.VMEM((full, 2 * HD), BF), pltpu.VMEM((HD, HD), BF)],
        (mate_lat, mats, shift, kg, q, acc), 2 * heads * full * full * 3 * HD, 2**22,
    )

    depth = heads * HD
    half = rows // 2
    rest, x_kept = call(
        functools.partial(stage_body, n_mp), "out_weights", (ids,), (n_mp,),
        [pl.BlockSpec((depth, d), lambda s, ids: (lax.rem(ids[2] + n_mp - ids[3 + s], n_mp), 0)),
         whole((ch, rows)), whole((ch, d))],
        [pl.BlockSpec((depth, d), lambda s, ids: (s, 0)), whole((half, d))],
        [jax.ShapeDtypeStruct((n_mp * depth, d), BF), jax.ShapeDtypeStruct((half, d), F32)], [],
        (w_out, lat_t, w_img_in), 2 * half * ch * d, 4 * n_mp * depth * d,
    )
    text_right, text_left, acc = lax.optimization_barrier((text_right, text_left, acc))
    text_far = ring(text_right, n_mp - 1)
    kv_near = text_kv("text_kv_near", text_left, text_right)
    mate_near = partner(kv_near, "group")

    scalars = (ids, txt_len, split_flag)
    acc = call(
        functools.partial(near_body, (0, n_mp - 1, 1), shard, n_mp), "text_attention_near", scalars, (heads,),
        [by_head(full, HD), by_head(full, 2 * HD)] + [by_head(v.shape[1], 2 * HD) for v in (kv_own, mate_own, kv_near, mate_near)],
        by_head(full, 2 * HD), jax.ShapeDtypeStruct(acc.shape, F32), [],
        (q, acc, kv_own, mate_own, kv_near, mate_near), 2 * heads * full * 6 * shard * 3 * HD, 2**23,
    )
    text_far, acc, rest = lax.optimization_barrier((text_far, acc, rest))
    kv_far = text_kv("text_kv_far", text_far)
    mate_far = partner(kv_far, "group")
    mixed = {}
    for name, steps in (("text_attention_far", order[1:2]), ("text_attention_rest", [*order[2:], order[0]])):
        out = call(
            functools.partial(last_body, (n_mp - 2,), shard, n_mp, steps), name, scalars, (1,),
            [VMEM] * 4, [VMEM] * (2 * len(steps)),
            [jax.ShapeDtypeStruct((half, depth), BF)] * (2 * len(steps)), [],
            (q, acc, kv_far, mate_far), heads * full * 2 * shard * 3 * HD, 2**22,
        )
        mixed.update({(s, flip): out[2 * i + flip] for i, s in enumerate(steps) for flip in range(2)})

    n_cfg = lax.axis_size("cfg")

    def send(s, flip):
        if s == 0 and flip == 0:
            return mixed[0, 0]
        pairs = [
            (c * n_mp + i, (c ^ flip) * n_mp + (i + s) % n_mp) for c in range(n_cfg) for i in range(n_mp)
        ]
        return lax.ppermute(mixed[s, flip], ("cfg", "mp"), pairs)

    pieces = {(s, flip): send(s, flip) for s in order[1:] + order[:1] for flip in range(2)}
    early = [pieces[s, flip] for s in order[:-1] for flip in range(2)]
    total = call(
        early_body, "out_early", (), (1,), [VMEM] * (len(early) + 1), VMEM,
        jax.ShapeDtypeStruct((rows, d), F32), [],
        (*early, rest), rows * len(early) * depth * d, len(early) * depth * d,
    )
    work = [pltpu.VMEM((half, d), F32), pltpu.VMEM((half, d), BF)]
    tables = (x_kept, mod_rows, mod_final, w_final.T)
    own_vel = call(
        own_body, "out_own", (ids, tstep), (1,), [VMEM] * 7, VMEM,
        jax.ShapeDtypeStruct((ch, half), F32), work,
        (total, pieces[order[-1], 0], rest, *tables), 2 * half * depth * d, 2 * depth * d,
    )
    vel, moved = call(
        out_body, "out_late", (ids, tstep, img_len, guide, step_size), (1,),
        [VMEM] * 9, [VMEM] * 2, [jax.ShapeDtypeStruct((1, ch, half), F32)] * 2, work,
        (total, pieces[order[-1], 1], rest, own_vel, lat_t, *tables), 2 * half * depth * d, 2 * depth * d,
    )
    return jnp.swapaxes(vel, 1, 2), jnp.swapaxes(moved, 1, 2)


def solution(mesh):
    placed = (
        P(("group", "mp"), None),
        P("cfg", ("group", "mp"), None),
        P(),
        P(None, "mp"),
        P(None, "mp"),
    ) + (P(),) * 13
    return jax.shard_map(
        local,
        mesh=mesh,
        in_specs=placed,
        out_specs=(P("cfg", ("group", "mp"), None), P("cfg", ("group", "mp"), None)),
        check_vma=False,
    )
```
